32 devices in a mesh: leaf: 2 (over core), prow: 4 (over y, x), pcol: 4 (over z).
Axes of the slice: x: 2, y: 2, z: 4, core: 2. Of those that a mesh axis runs over, the one named last changes fastest.
Arguments:
- child_inverse: float32 [32, 512, 512], P(('leaf', 'prow', 'pcol')), parts along dimension 0, as said below
- child_coupling: float32 [32, 1024, 512], P(('leaf', 'prow', 'pcol')), parts along dimension 0, may hold values from -0.25 to 0.25
- child_blocks: int32 [32], P(('leaf', 'prow', 'pcol')), parts along dimension 0, may hold values from 2 to 8, as said below
- child_map: int32 [32, 8], P(('leaf', 'prow', 'pcol')), parts along dimension 0, may hold values from -1 to 15, as said below
- parent_front: float32 [4096, 2048], P(('leaf', 'prow'), 'pcol'), parts along dimension 0, as said below
Outputs:
- parent_factored: float32 [4096, 2048], P(('leaf', 'prow'), 'pcol'), parts along dimension 0
The draws below stay inside these ranges and needn't reach their ends.
There are 2 independent parts, one for each index of `leaf`. The reference program is written for one: setup_inputs(seed, part) draws one part's arguments, and reference() takes and returns one part's arrays. A program takes and returns all parts, laid end to end along the dimension named above; each array names one. Nothing has to cross between parts.
Inputs may be any that keep to these rules, and one draw needn't show every extreme that they name: `child_inverse`: each matrix is lower triangular with a positive diagonal. `child_blocks`: the largest value 8 is taken by some child in every draw. `child_map`: in row c the first child_blocks[c] entries are distinct parent block ids in increasing order and the others are -1. `parent_front`: symmetric; the assembled front is positive definite.
All inputs are finite; a program needn't handle non-finite values.
Results may differ from the reference program's by a relative error of at most 0.0003.
Values sent between devices are 32-bit elements; how exact they have to be, the bound alone decides.
No kernel may reach another device: no remote copies, remote signals or barrier semaphores. Data moves between devices by JAX's collectives and lax.ppermute only.
A program may use at most 128 MiB of HBM per device.

```python
import math
import jax
import jax.numpy as jnp
from jax import lax

P_SIZE = 512
SMAX = 1024
BLK = 128
PORD = 2048
NCHILD = 16
PANEL = 512


def child_layout(key):
    folded = jax.random.fold_in(key, 7)
    slot_count = SMAX // BLK
    block_total = PORD // BLK
    blocks = jax.random.randint(jax.random.fold_in(folded, 1), (NCHILD,), 2, slot_count + 1)
    chosen = jax.random.randint(jax.random.fold_in(folded, 2), (), 0, NCHILD)
    blocks = jnp.where(jnp.arange(NCHILD) == chosen, slot_count, blocks)
    child_keys = jax.random.split(jax.random.fold_in(folded, 3), NCHILD)
    shuffled = jax.vmap(lambda one_key: jax.random.permutation(one_key, block_total))(child_keys)[:, :slot_count]
    in_use = jnp.arange(slot_count)[None, :] < blocks[:, None]
    sorted_ids = jnp.sort(jnp.where(in_use, shuffled, block_total), axis=1)
    mapping = jnp.where(sorted_ids < block_total, sorted_ids, -1)
    return (blocks.astype(jnp.int32), mapping.astype(jnp.int32))


def draw_child_blocks(key, part):
    return child_layout(key)[0]


def draw_child_map(key, part):
    return child_layout(key)[1]


def draw_child_inverse(key, part):
    first_key, second_key = jax.random.split(jax.random.fold_in(key, 11))
    raw_noise = jax.random.truncated_normal(first_key, -4.0, 4.0, (NCHILD, P_SIZE, P_SIZE), jnp.float32)
    diagonal = jnp.exp(jax.random.uniform(second_key, (NCHILD, P_SIZE), jnp.float32, math.log(0.35), math.log(0.65)))
    row_ids = jnp.arange(P_SIZE)[:, None]
    col_ids = jnp.arange(P_SIZE)[None, :]
    below = (row_ids > col_ids).astype(jnp.float32)
    identity = (row_ids == col_ids).astype(jnp.float32)
    return raw_noise * below[None, :, :] * (0.2 / math.sqrt(P_SIZE)) + identity[None, :, :] * diagonal[:, None, :]


def gram_front(key, order, gram_scale, low_ridge, high_ridge):
    first_key, second_key = jax.random.split(key)
    factor_noise = jax.random.truncated_normal(first_key, -4.0, 4.0, (order, order), jnp.float32)
    ridge = jnp.exp(jax.random.uniform(second_key, (order,), jnp.float32, math.log(low_ridge), math.log(high_ridge)))
    gram = jnp.dot(factor_noise, factor_noise.T, precision=lax.Precision.HIGHEST, preferred_element_type=jnp.float32) * (gram_scale / order)
    gram = 0.5 * (gram + gram.T)
    identity = jnp.eye(order, dtype=jnp.float32)
    return gram + identity * ridge[None, :]


def draw_parent_front(key, part):
    return gram_front(jax.random.fold_in(key, 13), PORD, 16.0, 4.0, 10.0)


def shard_levels(own_key, extent, cuts, least, top_value):
    loudness = 1.0
    for axis_at, parts in cuts:
        draws = jax.random.uniform(jax.random.fold_in(jax.random.fold_in(own_key, 6), axis_at), (parts,), jnp.float32, least / len(cuts), top_value / len(cuts))
        loudness = loudness * jnp.repeat(jnp.exp(draws), extent[axis_at] // parts).reshape((-1,) + (1,) * (len(extent) - 1 - axis_at))
    return loudness


def scatter_about(rng, extent, scale, bound, shards=(), kind=jnp.bfloat16):
    level = shard_levels(rng, extent, shards, -0.22, 0.18) if shards else 1.0
    entries = jax.random.normal(rng, extent, jnp.float32) * scale * level
    return jnp.minimum(jnp.maximum(entries, -bound), bound).astype(kind)


def setup_inputs(seed: int = 0, part: int = 0) -> dict:
    splits = jax.random.split(jax.random.key(seed), 6)
    part_splits = jax.random.split(jax.random.fold_in(splits[5], part), 6)
    return {
        "child_inverse": draw_child_inverse(jax.random.fold_in(jax.random.fold_in(splits[5], part), 71), part),
        "child_coupling": scatter_about(part_splits[1], (NCHILD, SMAX, P_SIZE), P_SIZE ** -0.5, 0.25, ((0, 16),), jnp.float32),
        "child_blocks": draw_child_blocks(jax.random.fold_in(jax.random.fold_in(splits[5], part), 71), part),
        "child_map": draw_child_map(jax.random.fold_in(jax.random.fold_in(splits[5], part), 71), part),
        "parent_front": draw_parent_front(jax.random.fold_in(jax.random.fold_in(splits[5], part), 71), part),
    }


def child_update(inverse_block, coupling, blocks, mapping):
    row_ids = jnp.arange(SMAX)
    masked = jnp.where((row_ids < blocks * BLK)[:, None], coupling, jnp.zeros_like(coupling))
    factor = jnp.dot(masked.astype(jnp.float32), inverse_block.T.astype(jnp.float32), precision=lax.Precision.HIGHEST, preferred_element_type=jnp.float32)
    update = jnp.dot(factor.astype(jnp.float32), factor.T.astype(jnp.float32), precision=lax.Precision.HIGHEST, preferred_element_type=jnp.float32)
    select = (mapping[None, :] == jnp.arange(PORD // BLK)[:, None]).astype(jnp.float32)
    blocked = update.reshape(SMAX // BLK, BLK, SMAX // BLK, BLK)
    spread = jnp.einsum('bk,kiln,dl->bidn', select, blocked, select, precision=lax.Precision.HIGHEST)
    return spread.reshape(PORD, PORD)

def reference(child_inverse, child_coupling, child_blocks, child_map, parent_front):

    def accumulate(summed, child_items):
        return (summed + child_update(*child_items), None)
    summed, unused = lax.scan(accumulate, jnp.zeros((PORD, PORD), jnp.float32), (child_inverse, child_coupling, child_blocks, child_map))
    assembled = parent_front - summed
    diag_factor = jnp.linalg.cholesky(assembled[:PANEL, :PANEL])
    solved = lax.linalg.triangular_solve(diag_factor, assembled[:, :PANEL], left_side=False, lower=True, transpose_a=True)
    panel_rows = jnp.concatenate([diag_factor, solved[PANEL:]], 0)
    below = panel_rows[PANEL:]
    trailing = assembled[PANEL:, PANEL:] - jnp.dot(below.astype(jnp.float32), below.T.astype(jnp.float32), precision=lax.Precision.HIGHEST, preferred_element_type=jnp.float32)
    upper_right = assembled[:PANEL, PANEL:]
    right_side = jnp.concatenate([upper_right, trailing], 0)
    return jnp.concatenate([panel_rows, right_side], 1)
```

```python
import functools
import itertools
import math

import jax
import jax.numpy as jnp
import numpy as np
from jax import lax
from jax.experimental import pallas as pl
from jax.experimental.pallas import tpu as pltpu
from jax.sharding import PartitionSpec as P

F32 = jnp.float32
BF16 = jnp.bfloat16
SMEM = pl.BlockSpec(memory_space=pltpu.SMEM)
VMEM = pl.BlockSpec(memory_space=pltpu.VMEM)
STRIDE = 256


class Plan:
    def __init__(self, rows, per_tile, slots):
        self.rows, self.per_tile, self.slots = rows, per_tile, slots
        nb = per_tile
        self.diag = [(a, a - s) for s in range(nb) for a in range(s, nb)]
        self.full = [(a, (a + s) % nb) for s in range(nb) for a in range(nb)]
        self.share = (len(self.diag) + 1) // 2
        self.extra = nb * nb - 2 * self.share
        self.pairs = [(h, l) for h in range(1, rows) for l in range(1, h)]
        self.column = max(nb * nb, len(self.pairs) * self.extra)
        self.length = self.column + (rows - 1) * self.share
        total = rows * nb
        table = -np.ones((total, total), np.int32)
        for h in range(1, rows):
            for a in range(nb):
                for b in range(nb):
                    table[h * nb + a, b] = h * STRIDE + a * nb + b
            for e, (a, b) in enumerate(self.diag):
                row = h if e < self.share else 0
                table[h * nb + a, h * nb + b] = row * STRIDE + self.chunk(h) + e % self.share
        for k, (h, l) in enumerate(self.pairs):
            for e, (a, b) in enumerate(self.full):
                if e < self.share:
                    code = h * STRIDE + self.chunk(l) + e
                elif e < 2 * self.share:
                    code = l * STRIDE + self.chunk(h) + e - self.share
                else:
                    code = k * self.extra + e - 2 * self.share
                table[h * nb + a, l * nb + b] = code
        self.table = table
        self.slot_pairs = [(i, j) for i in range(slots) for j in range(i + 1)]
        self.crossing = self.bound()

    def chunk(self, col):
        return self.column + (col - 1) * self.share

    def bound(self):
        total = self.table.shape[0]
        if math.comb(total, self.slots) > 100000:
            return len(self.slot_pairs)
        subsets = np.array(list(itertools.combinations(range(total), self.slots)))
        i, j = np.array(self.slot_pairs).T
        codes = self.table[subsets[:, i], subsets[:, j]]
        most = 0
        for bit in range(self.rows.bit_length() - 1):
            for value in range(2):
                hit = (codes >= 0) & ((codes // STRIDE >> bit) % 2 == value)
                most = max(most, int(hit.sum(1).max()))
        return most


def split(x):
    high = x.astype(BF16)
    return high, (x - high.astype(F32)).astype(BF16)


def dot3(a, b):
    dims = (((1,), (1,)), ((), ()))
    dot = lambda u, v: lax.dot_general(u, v, dims, preferred_element_type=F32)
    return dot(a[0], b[0]) + (dot(a[0], b[1]) + dot(a[1], b[0]))


def dot_nt(a, b):
    return lax.dot_general(
        a, b, (((1,), (1,)), ((), ())), precision=lax.Precision.HIGHEST, preferred_element_type=F32
    )


def dot_nn(a, b):
    return lax.dot_general(
        a, b, (((1,), (0,)), ((), ())), precision=lax.Precision.HIGHEST, preferred_element_type=F32
    )


def head_kernel(place, blocks, mapping, coupling, inverse, parent, out, *, blk, per_tile):
    count = per_tile * blk
    rows = lax.broadcasted_iota(jnp.int32, (count, 1), 0)
    masked = jnp.where(rows < blocks[0] * blk, coupling[...], 0.0)
    factor = split(dot3(split(masked), split(inverse[...])))
    update = dot3(factor, factor)
    lower = [(i, j) for j in range(per_tile) for i in range(j, per_tile)]
    own = (place[0] == 0) & (place[1] == 0)

    @pl.when(own)
    def _():
        for e, (i, j) in enumerate(lower):
            out[e * blk : (e + 1) * blk, :] = parent[i * blk : (i + 1) * blk, j * blk : (j + 1) * blk]

    @pl.when(jnp.logical_not(own))
    def _():
        out[...] = jnp.zeros_like(out)

    for i in range(per_tile):
        for j in range(i + 1):
            p, q = mapping[0, i], mapping[0, j]

            @pl.when((i < blocks[0]) & (p < per_tile))
            def _():
                place_at = q * per_tile - (q * (q - 1)) // 2 + p - q
                window = pl.ds(pl.multiple_of(place_at * blk, blk), blk)
                out[window, :] -= update[i * blk : (i + 1) * blk, j * blk : (j + 1) * blk]


def head(place, blocks, mapping, coupling, inverse, parent, blk, per_tile):
    count = per_tile * blk
    pivots = inverse.shape[0]
    n_lower = per_tile * (per_tile + 1) // 2
    return pl.pallas_call(
        functools.partial(head_kernel, blk=blk, per_tile=per_tile),
        grid=(1,),
        in_specs=[SMEM, SMEM, SMEM]
        + [
            pl.BlockSpec((count, pivots), lambda s: (0, 0)),
            pl.BlockSpec((pivots, pivots), lambda s: (0, 0)),
            pl.BlockSpec(parent.shape, lambda s: (0, 0)),
        ],
        out_specs=pl.BlockSpec((n_lower * blk, blk), lambda s: (0, 0)),
        out_shape=jax.ShapeDtypeStruct((n_lower * blk, blk), F32),
        compiler_params=pltpu.CompilerParams(vmem_limit_bytes=40 * 2**20),
    )(place, blocks, mapping, coupling, inverse, parent)


def lookup(e, slot_i, slot_j, blocks, mapping, table):
    i, j = slot_i[e], slot_j[e]
    p, q = jnp.maximum(mapping[0, i], 0), jnp.maximum(mapping[0, j], 0)
    code = table[p, q]
    return i, j, jnp.where(i < blocks[0], code, -1)


def pack_kernel(
    place, blocks, mapping, slot_i, slot_j, table, coupling, inverse, own, cross0, cross1, high, low, update, *, blk, plan
):
    half = blk // 2
    rows = lax.broadcasted_iota(jnp.int32, (coupling.shape[0], 1), 0)
    masked = jnp.where(rows < blocks[0] * blk, coupling[...], 0.0)
    high[...], low[...] = split(dot3(split(masked), split(inverse[...])))
    width = 2 * blk
    for start in range(0, coupling.shape[0], width):
        cols = slice(start, start + width)
        update[start:, cols] = dot3((high[start:, :], low[start:, :]), (high[cols, :], low[cols, :]))
    row = place[0]

    def tell(e):
        i, j, code = lookup(e, slot_i, slot_j, blocks, mapping, table)
        dest = code // STRIDE
        valid = code >= 0
        return i, j, valid, [valid & (((dest >> bit) ^ (row >> bit)) % 2 == 1) for bit in range(2)]

    def one(e, counts):
        i, j, valid, crosses = tell(e)
        upper = update[pl.ds(pl.multiple_of(i * blk, blk), half), pl.ds(pl.multiple_of(j * blk, blk), blk)]
        lower = update[pl.ds(pl.multiple_of(i * blk + half, half), half), pl.ds(pl.multiple_of(j * blk, blk), blk)]

        @pl.when(valid)
        def _():
            own[0, e] = -upper
            own[1, e] = -lower

        @pl.when(crosses[0])
        def _():
            cross0[counts[0]] = -upper

        @pl.when(crosses[1])
        def _():
            cross1[counts[1]] = -lower

        return tuple(c + x.astype(jnp.int32) for c, x in zip(counts, crosses))

    lax.fori_loop(0, len(plan.slot_pairs), one, (0, 0))


def pack(place, blocks, mapping, tables, coupling, inverse, blk, plan):
    half = blk // 2
    order, pivots = coupling.shape
    count = len(plan.slot_pairs)
    return pl.pallas_call(
        functools.partial(pack_kernel, blk=blk, plan=plan),
        in_specs=[SMEM] * 6 + [VMEM] * 2,
        out_specs=[VMEM] * 3,
        out_shape=[
            jax.ShapeDtypeStruct((2, count, half, blk), F32),
            jax.ShapeDtypeStruct((plan.crossing, half, blk), F32),
            jax.ShapeDtypeStruct((plan.crossing, half, blk), F32),
        ],
        scratch_shapes=[
            pltpu.VMEM((order, pivots), BF16),
            pltpu.VMEM((order, pivots), BF16),
            pltpu.VMEM((order, order), F32),
        ],
        compiler_params=pltpu.CompilerParams(vmem_limit_bytes=48 * 2**20),
    )(place, blocks, mapping, *tables, coupling, inverse)


def merge_kernel(
    place, blocks, mapping, blocks0, mapping0, blocks1, mapping1, slot_i, slot_j, table,
    own, cross0, cross1, parent, keep_out, send_out, both, *, blk, plan,
):
    half = blk // 2
    nb = plan.per_tile
    both[...] = jnp.zeros_like(both)
    row, col = place[0], place[1]
    mine = [row % 2, (row >> 1) % 2]

    @pl.when((col == 0) & (row > 0))
    def _():
        for a in range(nb):
            for b in range(nb):
                for h in range(2):
                    top = a * blk + h * half
                    both[0, h, a * nb + b] = parent[top : top + half, b * blk : (b + 1) * blk]

    def bits(code):
        dest = code // STRIDE
        return [dest % 2, (dest >> 1) % 2], code % STRIDE

    def add(h, other, index, value):
        both[other, h, index] += value

    def one(e, counts):
        _, _, code = lookup(e, slot_i, slot_j, blocks, mapping, table)
        bit, index = bits(code)
        for h in range(2):

            @pl.when((code >= 0) & (bit[h] == mine[h]))
            def _():
                add(h, bit[1 - h] ^ mine[1 - h], index, own[h, e])

        new = []
        for h, (b, m, got) in enumerate([(blocks0, mapping0, cross0), (blocks1, mapping1, cross1)]):
            _, _, code = lookup(e, slot_i, slot_j, b, m, table)
            bit, index = bits(code)
            hit = (code >= 0) & (bit[h] == mine[h])

            @pl.when(hit)
            def _():
                add(h, bit[1 - h] ^ mine[1 - h], index, got[counts[h]])

            new.append(counts[h] + hit.astype(jnp.int32))
        return tuple(new)

    lax.fori_loop(0, len(plan.slot_pairs), one, (0, 0))
    keep_out[...] = both[0]
    send_out[...] = both[1]


def merge(place, own_info, info0, info1, tables, own, cross0, cross1, parent, blk, plan):
    half = blk // 2
    shape = jax.ShapeDtypeStruct((2, plan.length, half, blk), F32)
    return pl.pallas_call(
        functools.partial(merge_kernel, blk=blk, plan=plan),
        in_specs=[SMEM] * 10 + [VMEM] * 4,
        out_specs=[VMEM] * 2,
        out_shape=[shape, shape],
        scratch_shapes=[pltpu.VMEM((2,) + shape.shape, F32)],
        compiler_params=pltpu.CompilerParams(vmem_limit_bytes=48 * 2**20),
    )(place, *own_info, *info0, *info1, *tables, own, cross0, cross1, parent)


def factor_block(a, u_ref, w_ref):
    n = a.shape[0]
    x = (lax.broadcasted_iota(jnp.int32, (n, n), 0) == lax.broadcasted_iota(jnp.int32, (n, n), 1)).astype(F32)
    step = 8
    for t in range(n // step):
        at, xt = a[:step], x[:step]
        cols = [jnp.broadcast_to(at[:, step * t + q : step * t + q + 1], at.shape) for q in range(step)]
        pivot = {(p, q): jnp.broadcast_to(cols[q][p : p + 1], at.shape) for q in range(step) for p in range(q, step)}
        scale, low = [], {}
        for q in range(step):
            scale.append(lax.rsqrt(pivot[q, q]))
            for p in range(q + 1, step):
                low[p, q] = pivot[p, q] * scale[q]
            for p in range(q + 1, step):
                for m in range(q + 1, p + 1):
                    pivot[p, m] = pivot[p, m] - low[p, q] * low[m, q]
        rows_a = [jnp.broadcast_to(at[q : q + 1], at.shape) for q in range(step)]
        rows_x = [jnp.broadcast_to(xt[q : q + 1], xt.shape) for q in range(step)]
        u, w = [], []
        for q in range(step):
            u.append(rows_a[q] * scale[q])
            w.append(rows_x[q] * scale[q])
            for p in range(q + 1, step):
                rows_a[p] = rows_a[p] - low[p, q] * u[q]
                rows_x[p] = rows_x[p] - low[p, q] * w[q]
            u_ref[step * t + q : step * t + q + 1, :] = u[q][:1]
            w_ref[step * t + q : step * t + q + 1, :] = w[q][:1]
        if t == n // step - 1:
            break
        for q in reversed(range(step)):
            u[q] = u[q] * scale[q]
            w[q] = w[q] * scale[q]
            for p in range(q):
                u[p] = u[p] - low[q, p] * u[q]
                w[p] = w[p] - low[q, p] * w[q]
        a, x = a[step:], x[step:]
        cols = [jnp.broadcast_to(a[:, step * t + q : step * t + q + 1], a.shape) for q in range(step)]
        for q in range(step):
            a = a - cols[q] * jnp.broadcast_to(u[q][:1], a.shape)
            x = x - cols[q] * jnp.broadcast_to(w[q][:1], x.shape)


def cholesky_kernel(place, lower, l_ref, x_ref, s, u_ref, w_ref, *, nb):
    n = l_ref.shape[0]
    tiles = n // nb
    part = lower.shape[1]
    at = {}
    e = 0
    for j in range(tiles):
        for i in range(j, tiles):
            at[i, j] = e
            e += 1
    flat = jnp.concatenate([lower[place[0] ^ d] for d in range(lower.shape[0])], 0)
    for (i, j), e in at.items():
        block = flat[e * nb : (e + 1) * nb, :]
        s[i * nb : (i + 1) * nb, j * nb : (j + 1) * nb] = block
        if i > j:
            s[j * nb : (j + 1) * nb, i * nb : (i + 1) * nb] = block.T
    rows = lax.broadcasted_iota(jnp.int32, (n, 1), 0)
    eye = lax.broadcasted_iota(jnp.int32, (n, n), 0) == lax.broadcasted_iota(jnp.int32, (n, n), 1)
    x_ref[...] = eye.astype(F32)
    tri = lax.broadcasted_iota(jnp.int32, (nb, nb), 0) >= lax.broadcasted_iota(jnp.int32, (nb, nb), 1)

    def step(k, _):
        off = pl.multiple_of(k * nb, nb)
        window = pl.ds(off, nb)
        factor_block(s[window, window], u_ref, w_ref)
        w = w_ref[...]
        below = jnp.where(rows >= off + nb, dot_nt(s[:, window], w), 0.0)
        l_ref[:, window] = below
        l_ref[window, window] = jnp.where(tri, u_ref[...].T, 0.0)
        xk = dot_nn(w, x_ref[window, :])
        s[...] -= dot_nt(below, below)
        x_ref[...] -= dot_nn(below, xk)
        x_ref[window, :] = xk
        return 0

    lax.fori_loop(0, tiles, step, 0)


def cholesky(place, lower, n, blk):
    return pl.pallas_call(
        functools.partial(cholesky_kernel, nb=blk),
        in_specs=[SMEM, VMEM],
        out_specs=[VMEM] * 2,
        out_shape=[jax.ShapeDtypeStruct((n, n), F32)] * 2,
        scratch_shapes=[pltpu.VMEM((n, n), F32), pltpu.VMEM((blk, blk), F32), pltpu.VMEM((blk, blk), F32)],
        compiler_params=pltpu.CompilerParams(vmem_limit_bytes=32 * 2**20),
    )(place, lower)


def finish_kernel(
    place, row_list, col_list, share_own, share_other, extra, parent, l_ref, x_ref, out, a_row, a_col, tile, *, blk, plan
):
    half = blk // 2
    nb = plan.per_tile
    row, col = place[0], place[1]

    def put(ref, a, b, upper, lower, sign=None):
        ref[a * blk : a * blk + half, b * blk : (b + 1) * blk] = upper
        ref[a * blk + half : (a + 1) * blk, b * blk : (b + 1) * blk] = lower

    for a in range(nb):
        for b in range(nb):
            put(a_col, a, b, col_list[0, a * nb + b], col_list[1, a * nb + b])

    @pl.when((row == 0) & (col == 0))
    def _():
        out[...] = l_ref[...]

    @pl.when((row == 0) & (col > 0))
    def _():
        out[...] = a_col[...].T

    @pl.when(row > 0)
    def _():
        for a in range(nb):
            for b in range(nb):
                put(a_row, a, b, row_list[0, a * nb + b], row_list[1, a * nb + b])
        a_row[...] = dot_nt(a_row[...], x_ref[...])

    @pl.when((row > 0) & (col == 0))
    def _():
        out[...] = a_row[...]

    @pl.when((row > 0) & (col == row))
    def _():
        for e, (a, b) in enumerate(plan.diag):
            src = share_own if e < plan.share else extra
            at = e % plan.share
            put(tile, a, b, src[0, at], src[1, at])
            if a > b:
                put(tile, b, a, *jnp.split(jnp.concatenate([src[0, at], src[1, at]], 0).T, 2, 0))
        pair = split(a_row[...])
        out[...] = parent[...] + tile[...] - dot3(pair, pair)

    @pl.when((row > 0) & (col > 0) & (col != row))
    def _():
        def fill(high_share, low_share):
            for e, (a, b) in enumerate(plan.full):
                src = [high_share, low_share, extra][min(e // plan.share, 2)]
                at = e - plan.share * min(e // plan.share, 2)
                put(tile, a, b, src[0, at], src[1, at])

        @pl.when(row > col)
        def _():
            fill(share_own, share_other)

        @pl.when(row < col)
        def _():
            fill(share_other, share_own)
            tile[...] = tile[...].T

        product = dot3(split(a_row[...]), split(dot_nt(a_col[...], x_ref[...])))
        out[...] = parent[...] + tile[...] - product


def finish(place, row_list, col_list, share_own, share_other, extra, parent, l, x, blk, plan):
    return pl.pallas_call(
        functools.partial(finish_kernel, blk=blk, plan=plan),
        in_specs=[SMEM] + [VMEM] * 8,
        out_specs=VMEM,
        out_shape=jax.ShapeDtypeStruct(parent.shape, F32),
        scratch_shapes=[pltpu.VMEM(parent.shape, F32)] * 3,
        compiler_params=pltpu.CompilerParams(vmem_limit_bytes=48 * 2**20),
    )(place, row_list, col_list, share_own, share_other, extra, parent, l, x)


def trade(x, axis, bit):
    size = lax.axis_size(axis)
    return lax.ppermute(x, axis, [(d, d ^ bit) for d in range(size)])


def shift(x, axis, by):
    size = lax.axis_size(axis)
    return lax.ppermute(x, axis, [(d, (d + by) % size) for d in range(size)])


def part(x, index, size):
    return lax.dynamic_slice_in_dim(x, index * size, size, 0)


def sum_head(lower):
    rows, cols = lax.axis_size("prow"), lax.axis_size("pcol")
    me = lax.axis_index("prow")
    size = lower.shape[0] // rows
    total = part(lower, me, size)
    for bit in range(1, rows):
        total = total + trade(part(lower, me ^ bit, size), "prow", bit)
    around = [shift(total, "pcol", by) for by in range(1, cols)]
    total = functools.reduce(jnp.add, around, total)
    return jnp.stack([total] + [trade(total, "prow", bit) for bit in range(1, rows)])


def ring_scatter(x, chunk_of):
    cols = lax.axis_size("pcol")
    me = lax.axis_index("pcol")
    total = chunk_of(x, (me - 1) % cols)
    for step in range(1, cols):
        total = shift(total, "pcol", 1) + chunk_of(x, (me - 1 - step) % cols)
    return total


def sum_column(x):
    cols = lax.axis_size("pcol")
    me = lax.axis_index("pcol")
    shape = x.shape
    flat = x.reshape(-1, shape[-1])
    size = flat.shape[0] // cols
    piece = ring_scatter(flat, lambda a, c: part(a, c, size))
    result = lax.dynamic_update_slice_in_dim(jnp.zeros_like(flat), piece, me * size, 0)
    for step in range(1, cols):
        piece = shift(piece, "pcol", 1)
        result = lax.dynamic_update_slice_in_dim(result, piece, (me - step) % cols * size, 0)
    return result.reshape(shape)


def spread_column(x):
    rows, cols = lax.axis_size("prow"), lax.axis_size("pcol")
    me, col = lax.axis_index("prow"), lax.axis_index("pcol")
    move = lambda v, pairs: lax.ppermute(v, ("prow", "pcol"), [(s * cols + c, d * cols + c) for s, d, c in pairs])
    planes = range(1, min(rows, cols))
    first = [move(x[h], [(c, c ^ (1 << h), c) for c in planes]) for h in range(2)]
    second = []
    got = jnp.stack(first)
    for h in range(2):
        src = jnp.where(me == col, x[h], first[h])
        over = 2 >> h
        second.append(
            move(src, [(c, c ^ over, c) for c in planes] + [(c ^ (1 << h), c ^ 3, c) for c in planes])
        )
    halves = []
    for h in range(2):
        near = me == col ^ (1 << h)
        halves.append(jnp.where(me == col, x[h], jnp.where(near, first[h], second[h])))
    return jnp.stack(halves)


def body(child_inverse, child_coupling, child_blocks, child_map, parent_front, plan):
    me, col = lax.axis_index("prow"), lax.axis_index("pcol")
    rows, cols = lax.axis_size("prow"), lax.axis_size("pcol")
    n = parent_front.shape[0]
    blk = child_coupling.shape[1] // child_map.shape[1]
    inverse, coupling = child_inverse[0], child_coupling[0]
    place = jnp.stack([me, col]).astype(jnp.int32)
    slot_i, slot_j = (jnp.asarray(np.array(plan.slot_pairs, np.int32).T[k]) for k in range(2))
    tables = (slot_i, slot_j, jnp.asarray(plan.table))
    info = (child_blocks, child_map)
    info0, info1 = (tuple(trade(v, "prow", bit) for v in info) for bit in (1, 2))

    lower = head(place, *info, coupling, inverse, parent_front, blk, plan.per_tile)
    summed_head = sum_head(lower)
    own, cross0, cross1 = pack(place, *info, tables, coupling, inverse, blk, plan)
    keep, send = merge(
        place, info, info0, info1, tables, own, trade(cross0, "prow", 1), trade(cross1, "prow", 2), parent_front, blk, plan
    )

    def second(cut):
        return jnp.stack([cut(keep[0]) + trade(cut(send[0]), "prow", 2), cut(keep[1]) + trade(cut(send[1]), "prow", 1)])

    column = sum_column(second(lambda v: v[: plan.column]))
    rest = second(lambda v: v[plan.column :])

    def chunk_of(x, c):
        return lax.dynamic_slice_in_dim(x, jnp.maximum(c - 1, 0) * plan.share, plan.share, 1)

    share_own = ring_scatter(rest, chunk_of)
    l, x = cholesky(place, summed_head, n, blk)
    col_list = spread_column(column)

    swap = [(r * cols + c, c * cols + r) for r in range(1, rows) for c in range(1, cols) if r != c]
    share_other = lax.ppermute(share_own, ("prow", "pcol"), swap)
    extra = jnp.zeros((2, plan.extra) + column.shape[2:], F32)
    pair_of = np.zeros((rows, cols), np.int32)
    for k, (h, l_) in enumerate(plan.pairs):
        pair_of[h, l_] = pair_of[l_, h] = k
    wide = jnp.pad(share_own, ((0, 0), (0, plan.extra - plan.share), (0, 0), (0, 0)))
    for r in range(1, rows):
        pair = jnp.asarray(pair_of[r])[col]
        piece = lax.dynamic_slice_in_dim(column, pair * plan.extra, plan.extra, 1)
        got = lax.ppermute(jnp.where(col == r, wide, piece), "prow", [(0, r)])
        extra = extra + got
    return finish(place, column, col_list, share_own, share_other, extra, parent_front, l, x, blk, plan)


def solution(mesh):
    def run(child_inverse, child_coupling, child_blocks, child_map, parent_front):
        rows = mesh.shape["prow"]
        slots = child_map.shape[1]
        blk = child_coupling.shape[1] // slots
        order = parent_front.shape[1]
        plan = Plan(rows, order // rows // blk, slots)
        return jax.shard_map(
            functools.partial(body, plan=plan),
            mesh=mesh,
            in_specs=(
                P(("leaf", "prow", "pcol"), None, None),
                P(("leaf", "prow", "pcol"), None, None),
                P(("leaf", "prow", "pcol")),
                P(("leaf", "prow", "pcol"), None),
                P(("leaf", "prow"), "pcol"),
            ),
            out_specs=P(("leaf", "prow"), "pcol"),
            check_vma=False,
        )(child_inverse, child_coupling, child_blocks, child_map, parent_front)

    return run
```

```python
import functools

import jax
import jax.numpy as jnp
import numpy as np
from jax import lax
from jax.experimental import pallas as pl
from jax.experimental.pallas import tpu as pltpu
from jax.sharding import Mesh
from jax.sharding import PartitionSpec as P

F32 = jnp.float32
BF16 = jnp.bfloat16
SMEM = pl.BlockSpec(memory_space=pltpu.SMEM)
VMEM = pl.BlockSpec(memory_space=pltpu.VMEM)
GROUP = ("prow", "near")


def vmem(megabytes):
    return pltpu.CompilerParams(vmem_limit_bytes=megabytes * 2**20)


class Plan:
    def __init__(self, rows, near, far, per_tile, slots, blk):
        self.rows, self.near, self.far = rows, near, far
        self.per_tile, self.slots, self.blk = per_tile, slots, blk
        self.members = rows * near
        self.strip = blk // self.members
        nb = per_tile
        self.lower = [(a, b) for b in range(nb) for a in range(b, nb)]
        self.full = [(a, b) for a in range(nb) for b in range(nb)]
        self.pairs = [(h, l) for h in range(1, rows) for l in range(1, h)]
        self.n_head = len(self.lower)
        self.n_column = (rows - 1) * nb * nb
        self.n_rest = (rows - 1) * len(self.lower) + len(self.pairs) * nb * nb
        self.total = self.n_head + self.n_column + self.n_rest
        self.slot_pairs = [(i, j) for j in range(slots) for i in range(j, slots)]
        table = np.full((rows * nb + 1, rows * nb + 1), self.total, np.int32)
        rest = self.n_head + self.n_column
        for r in range(rows):
            for e, (a, b) in enumerate(self.lower):
                at = e if r == 0 else rest + self.rest_at(r, r) + e
                table[r * nb + a + 1, r * nb + b + 1] = at
        for h in range(1, rows):
            for l in range(h):
                for e, (a, b) in enumerate(self.full):
                    at = self.n_head + (h - 1) * nb * nb + e if l == 0 else rest + self.rest_at(h, l) + e
                    table[h * nb + a + 1, l * nb + b + 1] = at
        self.table = table

    def rest_at(self, r, c):
        if r == 0 or c == 0:
            return 0
        if r == c:
            return (r - 1) * len(self.lower)
        k = self.pairs.index((max(r, c), min(r, c)))
        return (self.rows - 1) * len(self.lower) + k * len(self.full)


def split(x):
    high = x.astype(BF16)
    return high, (x - high.astype(F32)).astype(BF16)


def dot3(a, b):
    dims = (((1,), (1,)), ((), ()))
    dot = lambda u, v: lax.dot_general(u, v, dims, preferred_element_type=F32)
    return dot(a[0], b[0]) + (dot(a[0], b[1]) + dot(a[1], b[0]))


def dot_nt(a, b):
    return lax.dot_general(
        a, b, (((1,), (1,)), ((), ())), precision=lax.Precision.HIGHEST, preferred_element_type=F32
    )


def dot_nn(a, b):
    return lax.dot_general(
        a, b, (((1,), (0,)), ((), ())), precision=lax.Precision.HIGHEST, preferred_element_type=F32
    )


def parent_kernel(mapping, parent, out, *, plan):
    nb, blk, size = plan.per_tile, plan.blk, plan.strip
    lanes = lax.broadcasted_iota(jnp.int32, (size, blk), 1)
    coded = jnp.zeros((size, blk), F32)
    for s in range(plan.slots):
        coded = jnp.where(lanes == s, mapping[0, s].astype(F32), coded)
    for d in range(plan.members):
        for e, (a, b) in enumerate(plan.full):
            top = a * blk + d * size
            out[d, e] = parent[top : top + size, b * blk : (b + 1) * blk]
        out[d, len(plan.full)] = coded


def parent_strips(mapping, parent, plan):
    return pl.pallas_call(
        functools.partial(parent_kernel, plan=plan),
        in_specs=[SMEM, VMEM],
        out_specs=VMEM,
        out_shape=jax.ShapeDtypeStruct((plan.members, len(plan.full) + 1, plan.strip, plan.blk), F32),
        compiler_params=vmem(16),
    )(mapping, parent)


def update_kernel(blocks, coupling, inverse, out, high, low, update, *, plan):
    blk, size = plan.blk, plan.strip
    order = coupling.shape[0]
    rows = lax.broadcasted_iota(jnp.int32, (order, 1), 0)
    masked = jnp.where(rows < blocks[0] * blk, coupling[...], 0.0)
    high[...], low[...] = split(dot3(split(masked), split(inverse[...])))
    width = 2 * blk
    for start in range(0, order, width):
        cols = slice(start, start + width)
        update[start:, cols] = dot3((high[start:, :], low[start:, :]), (high[cols, :], low[cols, :]))
    for e, (i, j) in enumerate(plan.slot_pairs):
        for d in range(plan.members):
            top = i * blk + d * size
            out[d, e] = update[top : top + size, j * blk : (j + 1) * blk]


def update_strips(blocks, coupling, inverse, plan):
    order, pivots = coupling.shape
    shape = (plan.members, len(plan.slot_pairs), plan.strip, plan.blk)
    return pl.pallas_call(
        functools.partial(update_kernel, plan=plan),
        in_specs=[SMEM, VMEM, VMEM],
        out_specs=VMEM,
        out_shape=jax.ShapeDtypeStruct(shape, F32),
        scratch_shapes=[
            pltpu.VMEM((order, pivots), BF16),
            pltpu.VMEM((order, pivots), BF16),
            pltpu.VMEM((order, order), F32),
        ],
        compiler_params=vmem(40),
    )(blocks, coupling, inverse)


def merge_kernel(place, maps, table, strips, parents, head, column, rest, total, *, plan):
    nb = plan.per_tile
    total[...] = jnp.zeros_like(total)

    @pl.when(place[1] == 0)
    def _():
        for e, (a, b) in enumerate(plan.lower):
            total[e] = parents[0, a * nb + b]
        for r in range(1, plan.rows):
            for e in range(nb * nb):
                total[plan.n_head + (r - 1) * nb * nb + e] = parents[r * plan.near, e]

    def one(source, _):
        ids = [maps[source, s] + 1 for s in range(plan.slots)]
        for e, (i, j) in enumerate(plan.slot_pairs):
            at = table[ids[i], ids[j]]
            total[at] -= strips[source, e]
        return 0

    lax.fori_loop(0, plan.members, one, 0)
    head[...] = total[: plan.n_head]
    column[...] = total[plan.n_head : plan.n_head + plan.n_column]
    rest[...] = total[plan.n_head + plan.n_column : plan.total]


def merge(place, maps, strips, parents, plan):
    tail = (plan.strip, plan.blk)
    return pl.pallas_call(
        functools.partial(merge_kernel, plan=plan),
        in_specs=[SMEM] * 3 + [VMEM] * 2,
        out_specs=[VMEM] * 3,
        out_shape=[jax.ShapeDtypeStruct((n,) + tail, F32) for n in (plan.n_head, plan.n_column, plan.n_rest)],
        scratch_shapes=[pltpu.VMEM((plan.total + 1,) + tail, F32)],
        compiler_params=vmem(24),
    )(place, maps, jnp.asarray(plan.table), strips, parents)


def column_kernel(place, mine, other, out, total, *, plan):
    nb2 = len(plan.full)
    total[...] = mine[...] + other[...]
    for r in range(plan.rows):
        for n in range(plan.near):
            d = r * plan.near + n
            out[d, :nb2] = total[max(r - 1, 0) * nb2 : max(r - 1, 0) * nb2 + nb2]
            col = jnp.maximum(place[1] * plan.near + n - 1, 0)
            out[d, nb2:] = total[pl.ds(col * nb2, nb2)]


def column_strips(place, mine, other, plan):
    return pl.pallas_call(
        functools.partial(column_kernel, plan=plan),
        in_specs=[SMEM] + [VMEM] * 2,
        out_specs=VMEM,
        out_shape=jax.ShapeDtypeStruct((plan.members, 2 * len(plan.full)) + mine.shape[1:], F32),
        scratch_shapes=[pltpu.VMEM(mine.shape, F32)],
        compiler_params=vmem(16),
    )(place, mine, other)


def rest_kernel(place, starts, mine, other, out, total, *, plan):
    nb2 = len(plan.full)
    total[...] = mine[...] + other[...]
    for r in range(plan.rows):
        for n in range(plan.near):
            out[r * plan.near + n] = total[pl.ds(starts[place[1] * plan.near + n, r], nb2)]


def rest_strips(place, mine, other, plan):
    cols = plan.near * plan.far
    starts = np.array([[plan.rest_at(r, c) for r in range(plan.rows)] for c in range(cols)], np.int32)
    return pl.pallas_call(
        functools.partial(rest_kernel, plan=plan),
        in_specs=[SMEM] * 2 + [VMEM] * 2,
        out_specs=VMEM,
        out_shape=jax.ShapeDtypeStruct((plan.members, len(plan.full)) + mine.shape[1:], F32),
        scratch_shapes=[pltpu.VMEM(mine.shape, F32)],
        compiler_params=vmem(16),
    )(place, jnp.asarray(starts), mine, other)


def factor_block(a, u_ref, w_ref):
    n = a.shape[0]
    x = (lax.broadcasted_iota(jnp.int32, (n, n), 0) == lax.broadcasted_iota(jnp.int32, (n, n), 1)).astype(F32)
    step = 8
    for t in range(n // step):
        at, xt = a[:step], x[:step]
        cols = [jnp.broadcast_to(at[:, step * t + q : step * t + q + 1], at.shape) for q in range(step)]
        pivot = {(p, q): jnp.broadcast_to(cols[q][p : p + 1], at.shape) for q in range(step) for p in range(q, step)}
        scale, low = [], {}
        for q in range(step):
            scale.append(lax.rsqrt(pivot[q, q]))
            for p in range(q + 1, step):
                low[p, q] = pivot[p, q] * scale[q]
            for p in range(q + 1, step):
                for m in range(q + 1, p + 1):
                    pivot[p, m] = pivot[p, m] - low[p, q] * low[m, q]
        rows_a = [jnp.broadcast_to(at[q : q + 1], at.shape) for q in range(step)]
        rows_x = [jnp.broadcast_to(xt[q : q + 1], xt.shape) for q in range(step)]
        u, w = [], []
        for q in range(step):
            u.append(rows_a[q] * scale[q])
            w.append(rows_x[q] * scale[q])
            for p in range(q + 1, step):
                rows_a[p] = rows_a[p] - low[p, q] * u[q]
                rows_x[p] = rows_x[p] - low[p, q] * w[q]
            u_ref[step * t + q : step * t + q + 1, :] = u[q][:1]
            w_ref[step * t + q : step * t + q + 1, :] = w[q][:1]
        if t == n // step - 1:
            break
        for q in reversed(range(step)):
            u[q] = u[q] * scale[q]
            w[q] = w[q] * scale[q]
            for p in range(q):
                u[p] = u[p] - low[q, p] * u[q]
                w[p] = w[p] - low[q, p] * w[q]
        a, x = a[step:], x[step:]
        cols = [jnp.broadcast_to(a[:, step * t + q : step * t + q + 1], a.shape) for q in range(step)]
        for q in range(step):
            a = a - cols[q] * jnp.broadcast_to(u[q][:1], a.shape)
            x = x - cols[q] * jnp.broadcast_to(w[q][:1], x.shape)


def cholesky_kernel(lower, l_ref, x_ref, s, u_ref, w_ref, *, plan):
    n = l_ref.shape[0]
    nb = plan.blk
    size = plan.strip
    for e, (i, j) in enumerate(plan.lower):
        rows = slice(i * nb, (i + 1) * nb)
        cols = slice(j * nb, (j + 1) * nb)
        block = jnp.concatenate([lower[d, e] for d in range(plan.members)], 0)
        s[rows, cols] = block
        if i > j:
            s[cols, rows] = block.T
    rows = lax.broadcasted_iota(jnp.int32, (n, 1), 0)
    eye = lax.broadcasted_iota(jnp.int32, (n, n), 0) == lax.broadcasted_iota(jnp.int32, (n, n), 1)
    x_ref[...] = eye.astype(F32)
    tri = lax.broadcasted_iota(jnp.int32, (nb, nb), 0) >= lax.broadcasted_iota(jnp.int32, (nb, nb), 1)

    def step(k, _):
        off = pl.multiple_of(k * nb, nb)
        window = pl.ds(off, nb)
        factor_block(s[window, window], u_ref, w_ref)
        w = w_ref[...]
        below = jnp.where(rows >= off + nb, dot_nt(s[:, window], w), 0.0)
        l_ref[:, window] = below
        l_ref[window, window] = jnp.where(tri, u_ref[...].T, 0.0)
        xk = dot_nn(w, x_ref[window, :])
        s[...] -= dot_nt(below, below)
        x_ref[...] -= dot_nn(below, xk)
        x_ref[window, :] = xk
        return 0

    lax.fori_loop(0, n // nb, step, 0)


def cholesky(lower, n, plan):
    blk = plan.blk
    return pl.pallas_call(
        functools.partial(cholesky_kernel, plan=plan),
        in_specs=[VMEM],
        out_specs=[VMEM] * 2,
        out_shape=[jax.ShapeDtypeStruct((n, n), F32)] * 2,
        scratch_shapes=[pltpu.VMEM((n, n), F32), pltpu.VMEM((blk, blk), F32), pltpu.VMEM((blk, blk), F32)],
        compiler_params=vmem(24),
    )(lower)


def finish_kernel(place, columns, rests, parent, l_ref, x_ref, out, a_row, a_col, tile, *, plan):
    nb, blk, size = plan.per_tile, plan.blk, plan.strip
    nb2 = nb * nb
    row = place[0]
    col = place[1] * plan.near + place[2]

    def put(ref, source, first, blocks):
        for e, (a, b) in enumerate(blocks):
            for d in range(plan.members):
                top = a * blk + d * size
                ref[top : top + size, b * blk : (b + 1) * blk] = source[d, first + e]

    @pl.when((row == 0) & (col == 0))
    def _():
        out[...] = l_ref[...]

    @pl.when((row == 0) & (col > 0))
    def _():
        put(a_col, columns, nb2, plan.full)
        out[...] = a_col[...].T

    @pl.when(row > 0)
    def _():
        put(a_row, columns, 0, plan.full)
        a_row[...] = dot_nt(a_row[...], x_ref[...])

    @pl.when((row > 0) & (col == 0))
    def _():
        out[...] = a_row[...]

    @pl.when((row > 0) & (col == row))
    def _():
        put(tile, rests, 0, plan.lower)
        for a, b in plan.lower:
            if a > b:
                tile[b * blk : (b + 1) * blk, a * blk : (a + 1) * blk] = tile[
                    a * blk : (a + 1) * blk, b * blk : (b + 1) * blk
                ].T
        pair = split(a_row[...])
        out[...] = parent[...] + tile[...] - dot3(pair, pair)

    @pl.when((row > 0) & (col > 0) & (col != row))
    def _():
        put(a_col, columns, nb2, plan.full)
        put(tile, rests, 0, plan.full)

        @pl.when(row < col)
        def _():
            tile[...] = tile[...].T

        product = dot3(split(a_row[...]), split(dot_nt(a_col[...], x_ref[...])))
        out[...] = parent[...] + tile[...] - product


def finish(place, columns, rests, parent, l, x, plan):
    return pl.pallas_call(
        functools.partial(finish_kernel, plan=plan),
        in_specs=[SMEM] + [VMEM] * 5,
        out_specs=VMEM,
        out_shape=jax.ShapeDtypeStruct(parent.shape, F32),
        scratch_shapes=[pltpu.VMEM(parent.shape, F32)] * 3,
        compiler_params=vmem(32),
    )(place, columns, rests, parent, l, x)


def all_to_all(x):
    return lax.all_to_all(x, GROUP, 0, 0, tiled=True)


def across(x, plan):
    others = [
        lax.ppermute(x, "far", [(f, (f + by) % plan.far) for f in range(plan.far)]) for by in range(1, plan.far)
    ]
    return functools.reduce(jnp.add, others)


def body(child_inverse, child_coupling, child_blocks, child_map, parent_front, plan):
    place = jnp.stack([lax.axis_index(a) for a in ("prow", "far", "near")]).astype(jnp.int32)
    parents = all_to_all(parent_strips(child_map, parent_front, plan))
    maps = parents[:, len(plan.full), 0, : plan.slots].astype(jnp.int32)
    strips = all_to_all(update_strips(child_blocks, child_coupling[0], child_inverse[0], plan))
    head, column, rest = merge(place, maps, strips, parents, plan)
    head = head + across(head, plan)
    heads = all_to_all(jnp.broadcast_to(head, (plan.members,) + head.shape))
    l, x = cholesky(heads, parent_front.shape[0], plan)
    columns = all_to_all(column_strips(place, column, across(column, plan), plan))
    rests = all_to_all(rest_strips(place, rest, across(rest, plan), plan))
    return finish(place, columns, rests, parent_front, l, x, plan)


def solution(mesh):
    rows, cols = mesh.shape["prow"], mesh.shape["pcol"]
    near = 2 if cols % 2 == 0 else 1
    fine = Mesh(
        mesh.devices.reshape(mesh.shape["leaf"], rows, cols // near, near), ("leaf", "prow", "far", "near")
    )
    device = P(("leaf", "prow", "far", "near"))

    def run(child_inverse, child_coupling, child_blocks, child_map, parent_front):
        slots = child_map.shape[1]
        blk = child_coupling.shape[1] // slots
        plan = Plan(rows, near, cols // near, parent_front.shape[1] // cols // blk, slots, blk)
        tile = P(("leaf", "prow"), ("far", "near"))
        return jax.shard_map(
            functools.partial(body, plan=plan),
            mesh=fine,
            in_specs=(device, device, device, device, tile),
            out_specs=tile,
            check_vma=False,
        )(child_inverse, child_coupling, child_blocks, child_map, parent_front)

    return run
```

```python
import functools

import jax
import jax.numpy as jnp
import numpy as np
from jax import lax
from jax.experimental import pallas as pl
from jax.experimental.pallas import tpu as pltpu
from jax.sharding import Mesh
from jax.sharding import PartitionSpec as P

F32 = jnp.float32
BF16 = jnp.bfloat16
SMEM = pl.BlockSpec(memory_space=pltpu.SMEM)
VMEM = pl.BlockSpec(memory_space=pltpu.VMEM)
AFTER = pl.BlockSpec(memory_space=pl.ANY)
GROUP = ("prow", "near")


def vmem(megabytes):
    return pltpu.CompilerParams(vmem_limit_bytes=megabytes * 2**20)


class Plan:
    def __init__(self, rows, near, far, per_tile, slots, blk):
        self.rows, self.near, self.far = rows, near, far
        self.per_tile, self.slots, self.blk = per_tile, slots, blk
        self.members = rows * near
        self.strip = blk // self.members
        nb = per_tile
        self.lower = [(a, b) for b in range(nb) for a in range(b, nb)]
        self.full = [(a, b) for a in range(nb) for b in range(nb)]
        self.pairs = [(h, l) for h in range(1, rows) for l in range(1, h)]
        self.n_head = len(self.lower)
        self.n_column = (rows - 1) * nb * nb
        self.n_rest = (rows - 1) * len(self.lower) + len(self.pairs) * nb * nb
        self.total = self.n_head + self.n_column + self.n_rest
        self.first = len(self.full) // 2
        self.n_parent = max(len(self.lower), len(self.full) - self.first)
        self.slot_pairs = [(i, j) for j in range(slots) for i in range(j, slots)]
        table = np.full((rows * nb + 1, rows * nb + 1), self.total, np.int32)
        rest = self.n_head + self.n_column
        for r in range(rows):
            for e, (a, b) in enumerate(self.lower):
                at = e if r == 0 else rest + self.rest_at(r, r) + e
                table[r * nb + a + 1, r * nb + b + 1] = at
        for h in range(1, rows):
            for l in range(h):
                for e, (a, b) in enumerate(self.full):
                    at = self.n_head + (h - 1) * nb * nb + e if l == 0 else rest + self.rest_at(h, l) + e
                    table[h * nb + a + 1, l * nb + b + 1] = at
        self.table = table

    def rest_at(self, r, c):
        if r == 0 or c == 0:
            return 0
        if r == c:
            return (r - 1) * len(self.lower)
        k = self.pairs.index((max(r, c), min(r, c)))
        return (self.rows - 1) * len(self.lower) + k * len(self.full)


def split(x):
    high = x.astype(BF16)
    return high, (x - high.astype(F32)).astype(BF16)


def dot3(a, b):
    dims = (((1,), (1,)), ((), ()))
    dot = lambda u, v: lax.dot_general(u, v, dims, preferred_element_type=F32)
    return dot(a[0], b[0]) + (dot(a[0], b[1]) + dot(a[1], b[0]))


def dot_nt(a, b):
    return lax.dot_general(
        a, b, (((1,), (1,)), ((), ())), precision=lax.Precision.HIGHEST, preferred_element_type=F32
    )


def dot_nn(a, b):
    return lax.dot_general(
        a, b, (((1,), (0,)), ((), ())), precision=lax.Precision.HIGHEST, preferred_element_type=F32
    )


def update_kernel(place, blocks, mapping, coupling, inverse, parent, out, high, low, update, *, plan):
    blk, size = plan.blk, plan.strip
    order = coupling.shape[0]
    rows = lax.broadcasted_iota(jnp.int32, (order, 1), 0)
    masked = jnp.where(rows < blocks[0] * blk, coupling[...], 0.0)
    high[...], low[...] = split(dot3(split(masked), split(inverse[...])))
    width = 2 * blk
    for start in range(0, order, width):
        cols = slice(start, start + width)
        update[start:, cols] = dot3((high[start:, :], low[start:, :]), (high[cols, :], low[cols, :]))
    for e, (i, j) in enumerate(plan.slot_pairs):
        for d in range(plan.members):
            top = i * blk + d * size
            out[d, e] = update[top : top + size, j * blk : (j + 1) * blk]

    base = len(plan.slot_pairs)
    row, col = place[0], place[1] * plan.near + place[2]

    def send(blocks, transposed):
        for e, (a, b) in enumerate(blocks):
            p, q = (b, a) if transposed else (a, b)
            block = parent[p * blk : (p + 1) * blk, q * blk : (q + 1) * blk]
            block = block.T if transposed else block
            for d in range(plan.members):
                out[d, base + e] = block[d * size : (d + 1) * size]

    @pl.when((row == 0) & (col == 0))
    def _():
        send(plan.lower, False)

    @pl.when((row > 0) & (col == 0))
    def _():
        send(plan.full[: plan.first], False)

    @pl.when((row == 0) & (col > 0))
    def _():
        send(plan.full[plan.first :], True)

    lanes = lax.broadcasted_iota(jnp.int32, (size, blk), 1)
    coded = jnp.zeros((size, blk), F32)
    for s in range(plan.slots):
        coded = jnp.where(lanes == s, mapping[0, s].astype(F32), coded)
    for d in range(plan.members):
        out[d, base + plan.n_parent] = coded


def update_strips(place, blocks, mapping, coupling, inverse, parent, plan):
    order, pivots = coupling.shape
    shape = (plan.members, len(plan.slot_pairs) + plan.n_parent + 1, plan.strip, plan.blk)
    return pl.pallas_call(
        functools.partial(update_kernel, plan=plan),
        in_specs=[SMEM] * 3 + [VMEM] * 3,
        out_specs=VMEM,
        out_shape=jax.ShapeDtypeStruct(shape, F32),
        scratch_shapes=[
            pltpu.VMEM((order, pivots), BF16),
            pltpu.VMEM((order, pivots), BF16),
            pltpu.VMEM((order, order), F32),
        ],
        compiler_params=vmem(40),
    )(place, blocks, mapping, coupling, inverse, parent)


def merge_kernel(place, maps, table, strips, *refs, plan, rest):
    total = refs[-1]
    nb2 = len(plan.full)
    total[...] = jnp.zeros_like(total)
    if not rest:
        base = len(plan.slot_pairs)

        @pl.when(place[1] == 0)
        def _():
            for e in range(plan.n_head):
                total[e] = strips[0, base + e]
            for r in range(1, plan.rows):
                for e in range(plan.first):
                    total[plan.n_head + (r - 1) * nb2 + e] = strips[r * plan.near, base + e]

        for c in range(1, plan.rows):

            @pl.when(place[1] == c // plan.near)
            def _():
                for e in range(plan.first, nb2):
                    total[plan.n_head + (c - 1) * nb2 + e] = strips[c % plan.near, base + e - plan.first]

    def one(source, _):
        ids = [maps[source, s] + 1 for s in range(plan.slots)]
        for e, (i, j) in enumerate(plan.slot_pairs):
            at = table[ids[i], ids[j]]
            total[at] -= strips[source, e]
        return 0

    lax.fori_loop(0, plan.members, one, 0)
    if rest:
        refs[-2][...] = total[: plan.n_rest]
    else:
        refs[0][...] = total[: plan.n_head]
        refs[1][...] = total[plan.n_head : plan.n_head + plan.n_column]


def merge(place, maps, strips, plan, rest, after=()):
    tail = (plan.strip, plan.blk)
    begin = plan.n_head + plan.n_column
    if rest:
        counts = [plan.n_rest]
        table = np.where(plan.table >= begin, plan.table - begin, plan.n_rest)
    else:
        counts = [plan.n_head, plan.n_column]
        table = np.minimum(plan.table, begin)
    return pl.pallas_call(
        functools.partial(merge_kernel, plan=plan, rest=rest),
        in_specs=[SMEM] * 3 + [VMEM] + [AFTER] * len(after),
        out_specs=[VMEM] * len(counts),
        out_shape=[jax.ShapeDtypeStruct((n,) + tail, F32) for n in counts],
        scratch_shapes=[pltpu.VMEM((sum(counts) + 1,) + tail, F32)],
        compiler_params=vmem(24),
    )(place, maps, jnp.asarray(table.astype(np.int32)), strips, *after)


def column_kernel(place, mine, other, out, total, *, plan):
    nb2 = len(plan.full)
    total[...] = mine[...] + other[...]
    for r in range(plan.rows):
        for n in range(plan.near):
            d = r * plan.near + n
            out[d, :nb2] = total[max(r - 1, 0) * nb2 : max(r - 1, 0) * nb2 + nb2]
            col = jnp.maximum(place[1] * plan.near + n - 1, 0)
            out[d, nb2:] = total[pl.ds(col * nb2, nb2)]


def column_strips(place, mine, other, plan):
    return pl.pallas_call(
        functools.partial(column_kernel, plan=plan),
        in_specs=[SMEM] + [VMEM] * 2,
        out_specs=VMEM,
        out_shape=jax.ShapeDtypeStruct((plan.members, 2 * len(plan.full)) + mine.shape[1:], F32),
        scratch_shapes=[pltpu.VMEM(mine.shape, F32)],
        compiler_params=vmem(16),
    )(place, mine, other)


def rest_kernel(place, starts, mine, other, after, out, total, *, plan):
    nb2 = len(plan.full)
    total[...] = mine[...] + other[...]
    for r in range(plan.rows):
        for n in range(plan.near):
            out[r * plan.near + n] = total[pl.ds(starts[place[1] * plan.near + n, r], nb2)]


def rest_strips(place, mine, other, plan, after):
    cols = plan.near * plan.far
    starts = np.array([[plan.rest_at(r, c) for r in range(plan.rows)] for c in range(cols)], np.int32)
    return pl.pallas_call(
        functools.partial(rest_kernel, plan=plan),
        in_specs=[SMEM] * 2 + [VMEM] * 2 + [AFTER],
        out_specs=VMEM,
        out_shape=jax.ShapeDtypeStruct((plan.members, len(plan.full)) + mine.shape[1:], F32),
        scratch_shapes=[pltpu.VMEM(mine.shape, F32)],
        compiler_params=vmem(16),
    )(place, jnp.asarray(starts), mine, other, after)


def factor_block(a, u_ref, w_ref):
    n = a.shape[0]
    x = (lax.broadcasted_iota(jnp.int32, (n, n), 0) == lax.broadcasted_iota(jnp.int32, (n, n), 1)).astype(F32)
    step = 8
    for t in range(n // step):
        at, xt = a[:step], x[:step]
        cols = [jnp.broadcast_to(at[:, step * t + q : step * t + q + 1], at.shape) for q in range(step)]
        pivot = {(p, q): jnp.broadcast_to(cols[q][p : p + 1], at.shape) for q in range(step) for p in range(q, step)}
        scale, low = [], {}
        for q in range(step):
            scale.append(lax.rsqrt(pivot[q, q]))
            for p in range(q + 1, step):
                low[p, q] = pivot[p, q] * scale[q]
            for p in range(q + 1, step):
                for m in range(q + 1, p + 1):
                    pivot[p, m] = pivot[p, m] - low[p, q] * low[m, q]
        rows_a = [jnp.broadcast_to(at[q : q + 1], at.shape) for q in range(step)]
        rows_x = [jnp.broadcast_to(xt[q : q + 1], xt.shape) for q in range(step)]
        u, w = [], []
        for q in range(step):
            u.append(rows_a[q] * scale[q])
            w.append(rows_x[q] * scale[q])
            for p in range(q + 1, step):
                rows_a[p] = rows_a[p] - low[p, q] * u[q]
                rows_x[p] = rows_x[p] - low[p, q] * w[q]
            u_ref[step * t + q : step * t + q + 1, :] = u[q][:1]
            w_ref[step * t + q : step * t + q + 1, :] = w[q][:1]
        if t == n // step - 1:
            break
        for q in reversed(range(step)):
            u[q] = u[q] * scale[q]
            w[q] = w[q] * scale[q]
            for p in range(q):
                u[p] = u[p] - low[q, p] * u[q]
                w[p] = w[p] - low[q, p] * w[q]
        a, x = a[step:], x[step:]
        cols = [jnp.broadcast_to(a[:, step * t + q : step * t + q + 1], a.shape) for q in range(step)]
        for q in range(step):
            a = a - cols[q] * jnp.broadcast_to(u[q][:1], a.shape)
            x = x - cols[q] * jnp.broadcast_to(w[q][:1], x.shape)


def cholesky_kernel(lower, after, l_ref, x_ref, s, u_ref, w_ref, *, plan):
    n = l_ref.shape[0]
    nb = plan.blk
    size = plan.strip
    for e, (i, j) in enumerate(plan.lower):
        rows = slice(i * nb, (i + 1) * nb)
        cols = slice(j * nb, (j + 1) * nb)
        block = jnp.concatenate([lower[d, e] for d in range(plan.members)], 0)
        s[rows, cols] = block
        if i > j:
            s[cols, rows] = block.T
    rows = lax.broadcasted_iota(jnp.int32, (n, 1), 0)
    eye = lax.broadcasted_iota(jnp.int32, (n, n), 0) == lax.broadcasted_iota(jnp.int32, (n, n), 1)
    x_ref[...] = eye.astype(F32)
    tri = lax.broadcasted_iota(jnp.int32, (nb, nb), 0) >= lax.broadcasted_iota(jnp.int32, (nb, nb), 1)

    def step(k, _):
        off = pl.multiple_of(k * nb, nb)
        window = pl.ds(off, nb)
        factor_block(s[window, window], u_ref, w_ref)
        w = w_ref[...]
        below = jnp.where(rows >= off + nb, dot_nt(s[:, window], w), 0.0)
        l_ref[:, window] = below
        l_ref[window, window] = jnp.where(tri, u_ref[...].T, 0.0)
        xk = dot_nn(w, x_ref[window, :])
        s[...] -= dot_nt(below, below)
        x_ref[...] -= dot_nn(below, xk)
        x_ref[window, :] = xk
        return 0

    lax.fori_loop(0, n // nb, step, 0)


def cholesky(lower, n, plan, after):
    blk = plan.blk
    return pl.pallas_call(
        functools.partial(cholesky_kernel, plan=plan),
        in_specs=[VMEM, AFTER],
        out_specs=[VMEM] * 2,
        out_shape=[jax.ShapeDtypeStruct((n, n), F32)] * 2,
        scratch_shapes=[pltpu.VMEM((n, n), F32), pltpu.VMEM((blk, blk), F32), pltpu.VMEM((blk, blk), F32)],
        compiler_params=vmem(24),
    )(lower, after)


def put(ref, source, first, blocks, plan):
    blk, size = plan.blk, plan.strip
    for e, (a, b) in enumerate(blocks):
        for d in range(plan.members):
            top = a * blk + d * size
            ref[top : top + size, b * blk : (b + 1) * blk] = source[d, first + e]


def panel_kernel(place, columns, parent, l_ref, x_ref, out, a_row, a_col, *, plan):
    nb2 = len(plan.full)
    row = place[0]
    col = place[1] * plan.near + place[2]

    @pl.when((row == 0) & (col == 0))
    def _():
        out[...] = l_ref[...]

    @pl.when((row == 0) & (col > 0))
    def _():
        put(a_col, columns, nb2, plan.full, plan)
        out[...] = a_col[...].T

    @pl.when(row > 0)
    def _():
        put(a_row, columns, 0, plan.full, plan)
        a_row[...] = dot_nt(a_row[...], x_ref[...])

    @pl.when((row > 0) & (col == 0))
    def _():
        out[...] = a_row[...]

    @pl.when((row > 0) & (col == row))
    def _():
        pair = split(a_row[...])
        out[...] = parent[...] - dot3(pair, pair)

    @pl.when((row > 0) & (col > 0) & (col != row))
    def _():
        put(a_col, columns, nb2, plan.full, plan)
        out[...] = parent[...] - dot3(split(a_row[...]), split(dot_nt(a_col[...], x_ref[...])))


def panel(place, columns, parent, l, x, plan):
    return pl.pallas_call(
        functools.partial(panel_kernel, plan=plan),
        in_specs=[SMEM] + [VMEM] * 4,
        out_specs=VMEM,
        out_shape=jax.ShapeDtypeStruct(parent.shape, F32),
        scratch_shapes=[pltpu.VMEM(parent.shape, F32)] * 2,
        compiler_params=vmem(32),
    )(place, columns, parent, l, x)


def finish_kernel(place, rests, base, out, tile, *, plan):
    blk = plan.blk
    row = place[0]
    col = place[1] * plan.near + place[2]

    @pl.when((row == 0) | (col == 0))
    def _():
        out[...] = base[...]

    @pl.when((row > 0) & (col == row))
    def _():
        put(tile, rests, 0, plan.lower, plan)
        for a, b in plan.lower:
            if a > b:
                tile[b * blk : (b + 1) * blk, a * blk : (a + 1) * blk] = tile[
                    a * blk : (a + 1) * blk, b * blk : (b + 1) * blk
                ].T
        out[...] = base[...] + tile[...]

    @pl.when((row > col) & (col > 0))
    def _():
        put(tile, rests, 0, plan.full, plan)
        out[...] = base[...] + tile[...]

    @pl.when((row > 0) & (row < col))
    def _():
        put(tile, rests, 0, plan.full, plan)
        out[...] = base[...] + tile[...].T


def finish(place, rests, base, plan):
    return pl.pallas_call(
        functools.partial(finish_kernel, plan=plan),
        in_specs=[SMEM] + [VMEM] * 2,
        out_specs=VMEM,
        out_shape=jax.ShapeDtypeStruct(base.shape, F32),
        scratch_shapes=[pltpu.VMEM(base.shape, F32)],
        compiler_params=vmem(24),
    )(place, rests, base)


def all_to_all(x):
    return lax.all_to_all(x, GROUP, 0, 0, tiled=True)


def across(x, plan):
    others = [
        lax.ppermute(x, "far", [(f, (f + by) % plan.far) for f in range(plan.far)]) for by in range(1, plan.far)
    ]
    return functools.reduce(jnp.add, others)


def body(child_inverse, child_coupling, child_blocks, child_map, parent_front, plan):
    place = jnp.stack([lax.axis_index(a) for a in ("prow", "far", "near")]).astype(jnp.int32)
    strips = all_to_all(
        update_strips(place, child_blocks, child_map, child_coupling[0], child_inverse[0], parent_front, plan)
    )
    maps = strips[:, -1, 0, : plan.slots].astype(jnp.int32)
    head, column = merge(place, maps, strips, plan, False)
    head = head + across(head, plan)
    heads = all_to_all(jnp.broadcast_to(head, (plan.members,) + head.shape))
    (rest,) = merge(place, maps, strips, plan, True, (heads,))
    sent = column_strips(place, column, across(column, plan), plan)
    columns = all_to_all(sent)
    l, x = cholesky(heads, parent_front.shape[0], plan, sent)
    base = panel(place, columns, parent_front, l, x, plan)
    rests = all_to_all(rest_strips(place, rest, across(rest, plan), plan, l))
    return finish(place, rests, base, plan)


def solution(mesh):
    rows, cols = mesh.shape["prow"], mesh.shape["pcol"]
    near = 2 if cols % 2 == 0 else 1
    fine = Mesh(
        mesh.devices.reshape(mesh.shape["leaf"], rows, cols // near, near), ("leaf", "prow", "far", "near")
    )
    device = P(("leaf", "prow", "far", "near"))

    def run(child_inverse, child_coupling, child_blocks, child_map, parent_front):
        slots = child_map.shape[1]
        blk = child_coupling.shape[1] // slots
        plan = Plan(rows, near, cols // near, parent_front.shape[1] // cols // blk, slots, blk)
        tile = P(("leaf", "prow"), ("far", "near"))
        return jax.shard_map(
            functools.partial(body, plan=plan),
            mesh=fine,
            in_specs=(device, device, device, device, tile),
            out_specs=tile,
            check_vma=False,
        )(child_inverse, child_coupling, child_blocks, child_map, parent_front)

    return run
```

```python
import functools

import jax
import jax.numpy as jnp
import numpy as np
from jax import lax
from jax.experimental import pallas as pl
from jax.experimental.pallas import tpu as pltpu
from jax.sharding import Mesh
from jax.sharding import PartitionSpec as P

F32 = jnp.float32
BF16 = jnp.bfloat16
SMEM = pl.BlockSpec(memory_space=pltpu.SMEM)
VMEM = pl.BlockSpec(memory_space=pltpu.VMEM)
HBM = pl.BlockSpec(memory_space=pltpu.HBM)
AFTER = pl.BlockSpec(memory_space=pl.ANY)
GROUP = ("prow", "near")


def in_hbm(x):
    return pltpu.with_memory_space_constraint(x, pltpu.HBM)


def in_vmem(x):
    return pltpu.with_memory_space_constraint(x, pltpu.VMEM)


TOKEN = jax.ShapeDtypeStruct((8, 128), F32)


def call(kernel, megabytes, **kwargs):
    return pl.pallas_call(
        kernel,
        compiler_params=pltpu.CompilerParams(vmem_limit_bytes=megabytes * 2**20),
        cost_estimate=pl.CostEstimate(flops=1, bytes_accessed=1, transcendentals=0),
        **kwargs,
    )


class Plan:
    def __init__(self, rows, near, far, per_tile, slots, blk):
        self.rows, self.near, self.far = rows, near, far
        self.per_tile, self.slots, self.blk = per_tile, slots, blk
        self.members = rows * near
        self.strip = blk // self.members
        nb = per_tile
        self.lower = [(a, b) for b in range(nb) for a in range(b, nb)]
        self.full = [(a, b) for a in range(nb) for b in range(nb)]
        self.pairs = [(h, l) for h in range(1, rows) for l in range(1, h)]
        self.n_head = len(self.lower)
        self.n_column = (rows - 1) * nb * nb
        tiles = [(r, r) for r in range(1, rows)] + self.pairs
        need = {t: sorted({c // near for c in t}) for t in tiles}
        tiles.sort(key=lambda t: need[t])
        size = {t: len(self.lower) if t[0] == t[1] else nb * nb for t in tiles}
        self.starts = {t: sum(size[u] for u in tiles[:k]) for k, t in enumerate(tiles)}
        self.n_rest = sum(size.values())
        spans = []
        for f in range(far):
            held = [t for t in tiles if f in need[t]]
            spans.append((min(self.starts[t] for t in held), max(self.starts[t] + size[t] for t in held)))
        self.window = max(end - begin for begin, end in spans)
        self.begins = [min(begin, self.n_rest - self.window) for begin, _ in spans]
        self.total = self.n_head + self.n_column + self.n_rest
        self.first = len(self.full) // 2
        self.n_parent = max(len(self.lower), len(self.full) - self.first)
        self.slot_pairs = [(i, j) for j in range(slots) for i in range(j, slots)]
        self.early = sum(j < nb for _, j in self.slot_pairs)
        table = np.full((rows * nb + 1, rows * nb + 1), self.total, np.int32)
        rest = self.n_head + self.n_column
        for r in range(rows):
            for e, (a, b) in enumerate(self.lower):
                at = e if r == 0 else rest + self.rest_at(r, r) + e
                table[r * nb + a + 1, r * nb + b + 1] = at
        for h in range(1, rows):
            for l in range(h):
                for e, (a, b) in enumerate(self.full):
                    at = self.n_head + (h - 1) * nb * nb + e if l == 0 else rest + self.rest_at(h, l) + e
                    table[h * nb + a + 1, l * nb + b + 1] = at
        self.table = table

    def rest_at(self, r, c):
        if r == 0 or c == 0:
            return 0
        return self.starts[max(r, c), min(r, c)]


def split(x):
    high = x.astype(BF16)
    return high, (x - high.astype(F32)).astype(BF16)


def dot3(a, b):
    dims = (((1,), (1,)), ((), ()))
    dot = lambda u, v: lax.dot_general(u, v, dims, preferred_element_type=F32)
    return dot(a[0], b[0]) + (dot(a[0], b[1]) + dot(a[1], b[0]))


def dot_nt(a, b):
    return lax.dot_general(
        a, b, (((1,), (1,)), ((), ())), precision=lax.Precision.HIGHEST, preferred_element_type=F32
    )


def dot_nn(a, b):
    return lax.dot_general(
        a, b, (((1,), (0,)), ((), ())), precision=lax.Precision.HIGHEST, preferred_element_type=F32
    )


def update_kernel(
    place, blocks, mapping, coupling, inverse, parent, early, late, left, right, own, high, low, update, sems, *, plan
):
    blk, size = plan.blk, plan.strip
    order = coupling.shape[0]
    width = order // 2
    starts = [0, width]
    copies = [pltpu.make_async_copy(inverse, right, sems.at[0])]
    for k, start in enumerate(starts):
        window = pl.ds(start, width)
        copies.append(pltpu.make_async_copy(coupling.at[window], left.at[window], sems.at[k + 1]))
    copies.append(pltpu.make_async_copy(parent, own, sems.at[len(starts) + 1]))
    for copy in copies:
        copy.start()
    base = plan.early
    lanes = lax.broadcasted_iota(jnp.int32, (size, blk), 1)
    coded = jnp.zeros((size, blk), F32)
    for s in range(plan.slots):
        coded = jnp.where(lanes == s, mapping[0, s].astype(F32), coded)
    for d in range(plan.members):
        early[d, base + plan.n_parent] = coded
    copies[0].wait()
    factor_of = split(right[...])
    for k, start in enumerate(starts):
        window = slice(start, start + width)
        copies[k + 1].wait()
        rows = start + lax.broadcasted_iota(jnp.int32, (width, 1), 0)
        masked = jnp.where(rows < blocks[0] * blk, left[window, :], 0.0)
        high[window, :], low[window, :] = split(dot3(split(masked), factor_of))
    panel = 2 * blk
    for start in range(0, order, panel):
        cols = slice(start, start + panel)
        update[start:, cols] = dot3((high[start:, :], low[start:, :]), (high[cols, :], low[cols, :]))
    for e, (i, j) in enumerate(plan.slot_pairs):
        for d in range(plan.members):
            top = i * blk + d * size
            strip = update[top : top + size, j * blk : (j + 1) * blk]
            if e < plan.early:
                early[d, e] = strip
            else:
                late[d, e - plan.early] = strip

    copies[-1].wait()
    row, col = place[0], place[1] * plan.near + place[2]

    def send(blocks, transposed):
        for e, (a, b) in enumerate(blocks):
            p, q = (b, a) if transposed else (a, b)
            block = own[p * blk : (p + 1) * blk, q * blk : (q + 1) * blk]
            block = block.T if transposed else block
            for d in range(plan.members):
                early[d, base + e] = block[d * size : (d + 1) * size]

    @pl.when((row == 0) & (col == 0))
    def _():
        send(plan.lower, False)

    @pl.when((row > 0) & (col == 0))
    def _():
        send(plan.full[: plan.first], False)

    @pl.when((row == 0) & (col > 0))
    def _():
        send(plan.full[plan.first :], True)


def update_strips(place, blocks, mapping, coupling, inverse, parent, plan):
    order, pivots = coupling.shape
    counts = (plan.early + plan.n_parent + 1, len(plan.slot_pairs) - plan.early)
    return call(
        functools.partial(update_kernel, plan=plan),
        24,
        in_specs=[SMEM] * 3 + [HBM] * 3,
        out_specs=[VMEM] * 2,
        out_shape=[jax.ShapeDtypeStruct((plan.members, n, plan.strip, plan.blk), F32) for n in counts],
        scratch_shapes=[
            pltpu.VMEM(coupling.shape, F32),
            pltpu.VMEM(inverse.shape, F32),
            pltpu.VMEM(parent.shape, F32),
            pltpu.VMEM((order, pivots), BF16),
            pltpu.VMEM((order, pivots), BF16),
            pltpu.VMEM((order, order), F32),
            pltpu.SemaphoreType.DMA((4,)),
        ],
    )(place, blocks, mapping, *(in_hbm(v) for v in (coupling, inverse, parent)))


def merge_head_kernel(place, maps, table, early, head, token, total, *, plan):
    token[...] = jnp.zeros_like(token)
    base = plan.early

    @pl.when(place[1] == 0)
    def _():
        for e in range(plan.n_head):
            total[e] = early[0, base + e]

    @pl.when(place[1] != 0)
    def _():
        total[...] = jnp.zeros_like(total)

    def one(source, _):
        ids = [maps[source, s] + 1 for s in range(plan.per_tile)]
        for e, (i, j) in enumerate(plan.slot_pairs[: plan.early]):
            if i < plan.per_tile:
                total[table[ids[i], ids[j]]] -= early[source, e]
        return 0

    lax.fori_loop(0, plan.members, one, 0)
    head[...] = total[: plan.n_head]


def merge_head(place, maps, early, plan):
    tail = (plan.strip, plan.blk)
    table = np.minimum(plan.table, plan.n_head).astype(np.int32)
    return call(
        functools.partial(merge_head_kernel, plan=plan),
        6,
        in_specs=[SMEM] * 3 + [VMEM],
        out_specs=[VMEM] * 2,
        out_shape=[jax.ShapeDtypeStruct((plan.n_head,) + tail, F32), TOKEN],
        scratch_shapes=[pltpu.VMEM((plan.n_head + 1,) + tail, F32)],
    )(place, maps, jnp.asarray(table), early)


def merge_column_kernel(place, maps, table, early, after, column, total, *, plan):
    nb2 = len(plan.full)
    total[...] = jnp.zeros_like(total)
    base = plan.early

    @pl.when(place[1] == 0)
    def _():
        for r in range(1, plan.rows):
            for e in range(plan.first):
                total[(r - 1) * nb2 + e] = early[r * plan.near, base + e]

    for c in range(1, plan.rows):

        @pl.when(place[1] == c // plan.near)
        def _():
            for e in range(plan.first, nb2):
                total[(c - 1) * nb2 + e] = early[c % plan.near, base + e - plan.first]

    def one(source, _):
        ids = [maps[source, s] + 1 for s in range(plan.slots)]
        for e, (i, j) in enumerate(plan.slot_pairs[: plan.early]):
            if i > 0:
                total[table[ids[i], ids[j]]] -= early[source, e]
        return 0

    lax.fori_loop(0, plan.members, one, 0)
    column[...] = total[: plan.n_column]


def merge_column(place, maps, early, plan, after):
    tail = (plan.strip, plan.blk)
    first, last = plan.n_head, plan.n_head + plan.n_column
    inside = (plan.table >= first) & (plan.table < last)
    table = np.where(inside, plan.table - first, plan.n_column).astype(np.int32)
    return call(
        functools.partial(merge_column_kernel, plan=plan),
        8,
        in_specs=[SMEM] * 3 + [VMEM] + [AFTER],
        out_specs=VMEM,
        out_shape=jax.ShapeDtypeStruct((plan.n_column,) + tail, F32),
        scratch_shapes=[pltpu.VMEM((plan.n_column + 1,) + tail, F32)],
    )(place, maps, jnp.asarray(table), early, after)


def merge_rest_kernel(place, maps, table, begins, early, late, after, keep, send, token, total, *, plan):
    token[...] = jnp.zeros_like(token)
    total[...] = jnp.zeros_like(total)

    def one(source, _):
        ids = [maps[source, s] + 1 for s in range(plan.slots)]
        for e, (i, j) in enumerate(plan.slot_pairs):
            strip = early[source, e] if e < plan.early else late[source, e - plan.early]
            total[table[ids[i], ids[j]]] -= strip
        return 0

    lax.fori_loop(0, plan.members, one, 0)
    keep[...] = total[pl.ds(begins[place[1]], plan.window)]
    send[...] = total[pl.ds(begins[(place[1] + 1) % plan.far], plan.window)]


def merge_rest(place, maps, early, late, plan, after):
    first = plan.n_head + plan.n_column
    table = np.where(plan.table >= first, plan.table - first, plan.n_rest).astype(np.int32)
    shape = jax.ShapeDtypeStruct((plan.window, plan.strip, plan.blk), F32)
    return call(
        functools.partial(merge_rest_kernel, plan=plan),
        8,
        in_specs=[SMEM] * 4 + [VMEM] * 2 + [AFTER],
        out_specs=[VMEM] * 3,
        out_shape=[shape, shape, TOKEN],
        scratch_shapes=[pltpu.VMEM((plan.n_rest + 1, plan.strip, plan.blk), F32)],
    )(place, maps, jnp.asarray(table), jnp.asarray(np.array(plan.begins, np.int32)), early, late, after)


def column_kernel(place, mine, other, *refs, plan):
    sent, token, total, out, sems = refs[-5:]
    token[...] = jnp.zeros_like(token)
    nb2 = len(plan.full)
    total[...] = mine[...] + other[...]
    for r in range(plan.rows):
        for n in range(plan.near):
            d = r * plan.near + n
            out[d, :nb2] = total[max(r - 1, 0) * nb2 : max(r - 1, 0) * nb2 + nb2]
            col = jnp.maximum(place[1] * plan.near + n - 1, 0)
            out[d, nb2:] = total[pl.ds(col * nb2, nb2)]
            pltpu.make_async_copy(out.at[d], sent.at[d], sems.at[d]).start()
    for d in range(plan.members):
        pltpu.make_async_copy(out.at[d], sent.at[d], sems.at[d]).wait()


def column_strips(place, mine, other, plan, after):
    shape = (plan.members, 2 * len(plan.full)) + mine.shape[1:]
    return call(
        functools.partial(column_kernel, plan=plan),
        12,
        in_specs=[SMEM] + [VMEM] * 2 + [AFTER] * len(after),
        out_specs=[HBM, VMEM],
        out_shape=[pltpu.HBM(shape, F32), TOKEN],
        scratch_shapes=[
            pltpu.VMEM(mine.shape, F32),
            pltpu.VMEM(shape, F32),
            pltpu.SemaphoreType.DMA((plan.members,)),
        ],
    )(place, mine, other, *after)


def rest_kernel(place, starts, mine, other, after, out, token, total, *, plan):
    token[...] = jnp.zeros_like(token)
    nb2 = len(plan.full)
    total[...] = mine[...] + other[...]
    for r in range(plan.rows):
        for n in range(plan.near):
            out[r * plan.near + n] = total[pl.ds(starts[place[1] * plan.near + n, r], nb2)]


def rest_strips(place, mine, other, plan, after):
    cols = plan.near * plan.far
    nb2 = len(plan.full)
    starts = np.zeros((cols, plan.rows), np.int32)
    for c in range(1, cols):
        for r in range(1, plan.rows):
            starts[c, r] = min(plan.rest_at(r, c) - plan.begins[c // plan.near], plan.window - nb2)
    return call(
        functools.partial(rest_kernel, plan=plan),
        6,
        in_specs=[SMEM] * 2 + [VMEM] * 2 + [AFTER],
        out_specs=[VMEM] * 2,
        out_shape=[jax.ShapeDtypeStruct((plan.members, len(plan.full)) + mine.shape[1:], F32), TOKEN],
        scratch_shapes=[pltpu.VMEM(mine.shape, F32)],
    )(place, jnp.asarray(starts), mine, other, after)


def factor_block(a):
    step = 8
    count = a.shape[0] // step
    sub = lax.broadcasted_iota(jnp.int32, (step, a.shape[1]), 0)
    out = []
    for t in range(count):
        top = a[:step]
        row = lambda v, q: jnp.broadcast_to(v[q : q + 1], v.shape)
        col = lambda v, q: jnp.broadcast_to(v[:, step * t + q : step * t + q + 1], v.shape)
        cols = [col(top, q) for q in range(step)]
        pivot = {(p, q): row(cols[q], p) for q in range(step) for p in range(q, step)}
        scale, low = [], {}
        for q in range(step):
            scale.append(lax.rsqrt(pivot[q, q]))
            for p in range(q + 1, step):
                low[p, q] = pivot[p, q] * scale[q]
            for p in range(q + 1, step):
                for m in range(q + 1, p + 1):
                    pivot[p, m] = pivot[p, m] - low[p, q] * low[m, q]
        rows = [row(top, q) for q in range(step)]
        u = []
        for q in range(step):
            u.append(rows[q] * scale[q])
            for p in range(q + 1, step):
                rows[p] = rows[p] - low[p, q] * u[q]
        done = u[0]
        for q in range(1, step):
            done = jnp.where(sub == q, u[q], done)
        out.append(done)
        if t == count - 1:
            break
        for q in reversed(range(step)):
            u[q] = u[q] * scale[q]
            for p in range(q):
                u[p] = u[p] - low[q, p] * u[q]
        a = a[step:]
        cols = [col(a, q) for q in range(step)]
        for q in range(step):
            a = a - cols[q] * jnp.broadcast_to(u[q][:1], a.shape)
    return jnp.concatenate(out, 0)


def cholesky_kernel(place, *refs, plan):
    heads, (l_ref, x_ref, token, s) = refs[: plan.rows], refs[-4:]
    token[...] = jnp.zeros_like(token)
    n = l_ref.shape[0]
    blk, nb = plan.blk, plan.blk // 2
    l_ref[...] = jnp.zeros_like(l_ref)
    x_ref[...] = jnp.zeros_like(x_ref)
    for k, ref in enumerate(heads):
        for m in range(plan.near):
            member = (place[0] ^ k) * plan.near + (place[2] ^ m)
            for e, (i, j) in enumerate(plan.lower):
                top = pl.multiple_of(i * blk + member * plan.strip, plan.strip)
                s[pl.ds(top, plan.strip), j * blk : (j + 1) * blk] = ref[m, e]
    for i, j in plan.lower:
        if i > j:
            s[j * blk : (j + 1) * blk, i * blk : (i + 1) * blk] = s[i * blk : (i + 1) * blk, j * blk : (j + 1) * blk].T
    r, c = (lax.broadcasted_iota(jnp.int32, (nb, nb), d) for d in range(2))
    for off in range(0, n, nb):
        end = off + nb
        both = factor_block(jnp.concatenate([s[off:end, off:end], (r == c).astype(F32)], 1))
        w = both[:, nb:]
        l_ref[off:end, off:end] = jnp.where(r >= c, both[:, :nb].T, 0.0)
        x_ref[off:end, off:end] = w
        if off:
            x_ref[off:end, :off] = dot_nn(w, x_ref[off:end, :off])
        if end < n:
            below = dot_nt(s[end:, off:end], w)
            s[end:, end:] -= dot_nt(below, below)
            l_ref[end:, off:end] = below
            x_ref[end:, :end] -= dot_nn(below, x_ref[off:end, :end])


def cholesky(place, heads, n, plan, after):
    square = jax.ShapeDtypeStruct((n, n), F32)
    return call(
        functools.partial(cholesky_kernel, plan=plan),
        12,
        in_specs=[SMEM] + [VMEM] * plan.rows + [AFTER],
        out_specs=[VMEM] * 3,
        out_shape=[square, square, TOKEN],
        scratch_shapes=[pltpu.VMEM((n, n), F32)],
    )(place, *heads, after)


def put(ref, source, first, blocks, plan):
    blk, size = plan.blk, plan.strip
    for e, (a, b) in enumerate(blocks):
        for d in range(plan.members):
            top = a * blk + d * size
            ref[top : top + size, b * blk : (b + 1) * blk] = source[d, first + e]


def panel_kernel(place, columns, parent, l_ref, x_ref, after, out, a_row, a_col, *, plan):
    nb2 = len(plan.full)
    row = place[0]
    col = place[1] * plan.near + place[2]

    @pl.when((row == 0) & (col == 0))
    def _():
        out[...] = l_ref[...]

    @pl.when((row == 0) & (col > 0))
    def _():
        put(a_col, columns, nb2, plan.full, plan)
        out[...] = a_col[...].T

    @pl.when(row > 0)
    def _():
        put(a_row, columns, 0, plan.full, plan)
        a_row[...] = dot_nt(a_row[...], x_ref[...])

    @pl.when((row > 0) & (col == 0))
    def _():
        out[...] = a_row[...]

    @pl.when((row > 0) & (col == row))
    def _():
        pair = split(a_row[...])
        out[...] = parent[...] - dot3(pair, pair)

    @pl.when((row > 0) & (col > 0) & (col != row))
    def _():
        put(a_col, columns, nb2, plan.full, plan)
        out[...] = parent[...] - dot3(split(a_row[...]), split(dot_nt(a_col[...], x_ref[...])))


def panel(place, columns, parent, l, x, plan, after):
    return call(
        functools.partial(panel_kernel, plan=plan),
        12,
        in_specs=[SMEM] + [VMEM] * 4 + [AFTER],
        out_specs=VMEM,
        out_shape=jax.ShapeDtypeStruct(parent.shape, F32),
        scratch_shapes=[pltpu.VMEM(parent.shape, F32)] * 2,
    )(place, columns, parent, l, x, after)


def finish_kernel(place, rests_in, base_in, out, tile, rests, base, sems, *, plan):
    blk = plan.blk
    copies = [pltpu.make_async_copy(rests_in, rests, sems.at[0]), pltpu.make_async_copy(base_in, base, sems.at[1])]
    for copy in copies:
        copy.start()
    for copy in copies:
        copy.wait()
    row = place[0]
    col = place[1] * plan.near + place[2]

    @pl.when((row == 0) | (col == 0))
    def _():
        out[...] = base[...]

    @pl.when((row > 0) & (col == row))
    def _():
        put(tile, rests, 0, plan.lower, plan)
        for a, b in plan.lower:
            if a > b:
                tile[b * blk : (b + 1) * blk, a * blk : (a + 1) * blk] = tile[
                    a * blk : (a + 1) * blk, b * blk : (b + 1) * blk
                ].T
        out[...] = base[...] + tile[...]

    @pl.when((row > col) & (col > 0))
    def _():
        put(tile, rests, 0, plan.full, plan)
        out[...] = base[...] + tile[...]

    @pl.when((row > 0) & (row < col))
    def _():
        put(tile, rests, 0, plan.full, plan)
        out[...] = base[...] + tile[...].T


def finish(place, rests, base, plan):
    return call(
        functools.partial(finish_kernel, plan=plan),
        10,
        in_specs=[SMEM] + [HBM] * 2,
        out_specs=VMEM,
        out_shape=jax.ShapeDtypeStruct(base.shape, F32),
        scratch_shapes=[
            pltpu.VMEM(base.shape, F32),
            pltpu.VMEM(rests.shape, F32),
            pltpu.VMEM(base.shape, F32),
            pltpu.SemaphoreType.DMA((2,)),
        ],
    )(place, in_hbm(rests), in_hbm(base))


def all_to_all(x):
    return lax.all_to_all(x, GROUP, 0, 0, tiled=True)


def across(x, plan):
    others = [
        lax.ppermute(x, "far", [(f, (f + by) % plan.far) for f in range(plan.far)]) for by in range(1, plan.far)
    ]
    return functools.reduce(jnp.add, others)


def spread_head(head, plan):
    cols = plan.near * plan.far
    got = [head] + [lax.ppermute(head, ("far", "near"), [(d, d ^ k) for d in range(cols)]) for k in range(1, cols)]
    pair = jnp.stack([sum(got[m + plan.near :: plan.near], got[m]) for m in range(plan.near)])
    return [pair] + [lax.ppermute(pair, "prow", [(d, d ^ k) for d in range(plan.rows)]) for k in range(1, plan.rows)]


def body(child_inverse, child_coupling, child_blocks, child_map, parent_front, plan):
    place = jnp.stack([lax.axis_index(a) for a in ("prow", "far", "near")]).astype(jnp.int32)
    early, late = update_strips(
        place, child_blocks, child_map, child_coupling[0], child_inverse[0], parent_front, plan
    )
    early = all_to_all(early)
    late = all_to_all(late)
    maps = early[:, -1, 0, : plan.slots].astype(jnp.int32)
    head, token = merge_head(place, maps, early, plan)
    heads = spread_head(head, plan)
    column = merge_column(place, maps, early, plan, token)
    far_column = across(column, plan)
    keep, send, token = merge_rest(place, maps, early, late, plan, heads[0])
    sent, token = column_strips(place, column, far_column, plan, [token] + heads[1:])
    columns = all_to_all(sent)
    l, x, token = cholesky(place, heads, parent_front.shape[0], plan, token)
    sent, token = rest_strips(place, keep, across(send, plan), plan, token)
    base = panel(place, columns, parent_front, l, x, plan, token)
    rests = all_to_all(sent)
    return finish(place, rests, base, plan)


def solution(mesh):
    rows, cols = mesh.shape["prow"], mesh.shape["pcol"]
    near = 2 if cols % 2 == 0 else 1
    fine = Mesh(
        mesh.devices.reshape(mesh.shape["leaf"], rows, cols // near, near), ("leaf", "prow", "far", "near")
    )
    device = P(("leaf", "prow", "far", "near"))

    def run(child_inverse, child_coupling, child_blocks, child_map, parent_front):
        slots = child_map.shape[1]
        blk = child_coupling.shape[1] // slots
        plan = Plan(rows, near, cols // near, parent_front.shape[1] // cols // blk, slots, blk)
        tile = P(("leaf", "prow"), ("far", "near"))
        return jax.shard_map(
            functools.partial(body, plan=plan),
            mesh=fine,
            in_specs=(device, device, device, device, tile),
            out_specs=tile,
            check_vma=False,
        )(child_inverse, child_coupling, child_blocks, child_map, parent_front)

    return run
```

```python
import functools

import jax
import jax.numpy as jnp
import numpy as np
from jax import lax
from jax.experimental import pallas as pl
from jax.experimental.pallas import tpu as pltpu
from jax.sharding import Mesh
from jax.sharding import PartitionSpec as P

F32 = jnp.float32
BF16 = jnp.bfloat16
SMEM = pl.BlockSpec(memory_space=pltpu.SMEM)
VMEM = pl.BlockSpec(memory_space=pltpu.VMEM)
HBM = pl.BlockSpec(memory_space=pltpu.HBM)
AFTER = pl.BlockSpec(memory_space=pl.ANY)
GROUP = ("prow", "near")


def in_hbm(x):
    return pltpu.with_memory_space_constraint(x, pltpu.HBM)


def in_vmem(x):
    return pltpu.with_memory_space_constraint(x, pltpu.VMEM)


TOKEN = jax.ShapeDtypeStruct((8, 128), F32)


def call(kernel, megabytes, **kwargs):
    return pl.pallas_call(
        kernel,
        compiler_params=pltpu.CompilerParams(vmem_limit_bytes=megabytes * 2**20),
        cost_estimate=pl.CostEstimate(flops=1, bytes_accessed=1, transcendentals=0),
        **kwargs,
    )


class Plan:
    def __init__(self, rows, near, far, per_tile, slots, blk):
        self.rows, self.near, self.far = rows, near, far
        self.per_tile, self.slots, self.blk = per_tile, slots, blk
        self.members = rows * near
        self.strip = blk // self.members
        nb = per_tile
        self.lower = [(a, b) for b in range(nb) for a in range(b, nb)]
        self.full = [(a, b) for a in range(nb) for b in range(nb)]
        self.pairs = [(h, l) for h in range(1, rows) for l in range(1, h)]
        self.n_head = len(self.lower)
        self.n_column = (rows - 1) * nb * nb
        tiles = [(r, r) for r in range(1, rows)] + self.pairs
        need = {t: sorted({c // near for c in t}) for t in tiles}
        tiles.sort(key=lambda t: need[t])
        size = {t: len(self.lower) if t[0] == t[1] else nb * nb for t in tiles}
        self.starts = {t: sum(size[u] for u in tiles[:k]) for k, t in enumerate(tiles)}
        self.n_rest = sum(size.values())
        spans = []
        for f in range(far):
            held = [t for t in tiles if f in need[t]]
            spans.append((min(self.starts[t] for t in held), max(self.starts[t] + size[t] for t in held)))
        self.window = max(end - begin for begin, end in spans)
        self.begins = [min(begin, self.n_rest - self.window) for begin, _ in spans]
        self.total = self.n_head + self.n_column + self.n_rest
        self.first = len(self.full) // 2
        self.n_parent = max(len(self.lower), len(self.full) - self.first)
        self.slot_pairs = [(i, j) for j in range(slots) for i in range(j, slots)]
        self.early = sum(j < nb for _, j in self.slot_pairs)
        table = np.full((rows * nb + 1, rows * nb + 1), self.total, np.int32)
        rest = self.n_head + self.n_column
        for r in range(rows):
            for e, (a, b) in enumerate(self.lower):
                at = e if r == 0 else rest + self.rest_at(r, r) + e
                table[r * nb + a + 1, r * nb + b + 1] = at
        for h in range(1, rows):
            for l in range(h):
                for e, (a, b) in enumerate(self.full):
                    at = self.n_head + (h - 1) * nb * nb + e if l == 0 else rest + self.rest_at(h, l) + e
                    table[h * nb + a + 1, l * nb + b + 1] = at
        self.table = table

    def rest_at(self, r, c):
        if r == 0 or c == 0:
            return 0
        return self.starts[max(r, c), min(r, c)]


def split(x):
    high = x.astype(BF16)
    return high, (x - high.astype(F32)).astype(BF16)


def dot3(a, b):
    dims = (((1,), (1,)), ((), ()))
    dot = lambda u, v: lax.dot_general(u, v, dims, preferred_element_type=F32)
    return dot(a[0], b[0]) + (dot(a[0], b[1]) + dot(a[1], b[0]))


def dot_nt(a, b):
    return lax.dot_general(
        a, b, (((1,), (1,)), ((), ())), precision=lax.Precision.HIGHEST, preferred_element_type=F32
    )


def dot_nn(a, b):
    return lax.dot_general(
        a, b, (((1,), (0,)), ((), ())), precision=lax.Precision.HIGHEST, preferred_element_type=F32
    )


def update_kernel(
    place, blocks, mapping, coupling, inverse, parent, early, late, left, right, own, high, low, update, sems, *, plan
):
    blk, size = plan.blk, plan.strip
    order = coupling.shape[0]
    width = order // 2
    starts = [0, width]
    copies = [pltpu.make_async_copy(inverse, right, sems.at[0])]
    for k, start in enumerate(starts):
        window = pl.ds(start, width)
        copies.append(pltpu.make_async_copy(coupling.at[window], left.at[window], sems.at[k + 1]))
    copies.append(pltpu.make_async_copy(parent, own, sems.at[len(starts) + 1]))
    for copy in copies:
        copy.start()
    base = plan.early
    lanes = lax.broadcasted_iota(jnp.int32, (size, blk), 1)
    coded = jnp.zeros((size, blk), F32)
    for s in range(plan.slots):
        coded = jnp.where(lanes == s, mapping[0, s].astype(F32), coded)
    for d in range(plan.members):
        early[d, base + plan.n_parent] = coded
    copies[0].wait()
    factor_of = split(right[...])
    for k, start in enumerate(starts):
        window = slice(start, start + width)
        copies[k + 1].wait()
        rows = start + lax.broadcasted_iota(jnp.int32, (width, 1), 0)
        masked = jnp.where(rows < blocks[0] * blk, left[window, :], 0.0)
        high[window, :], low[window, :] = split(dot3(split(masked), factor_of))
    panel = 2 * blk
    for start in range(0, order, panel):
        cols = slice(start, start + panel)
        update[start:, cols] = dot3((high[start:, :], low[start:, :]), (high[cols, :], low[cols, :]))
    for e, (i, j) in enumerate(plan.slot_pairs):
        for d in range(plan.members):
            top = i * blk + d * size
            strip = update[top : top + size, j * blk : (j + 1) * blk]
            if e < plan.early:
                early[d, e] = strip
            else:
                late[d, e - plan.early] = strip

    copies[-1].wait()
    row, col = place[0], place[1] * plan.near + place[2]

    def send(blocks, transposed):
        for e, (a, b) in enumerate(blocks):
            p, q = (b, a) if transposed else (a, b)
            block = own[p * blk : (p + 1) * blk, q * blk : (q + 1) * blk]
            block = block.T if transposed else block
            for d in range(plan.members):
                early[d, base + e] = block[d * size : (d + 1) * size]

    @pl.when((row == 0) & (col == 0))
    def _():
        send(plan.lower, False)

    @pl.when((row > 0) & (col == 0))
    def _():
        send(plan.full[: plan.first], False)

    @pl.when((row == 0) & (col > 0))
    def _():
        send(plan.full[plan.first :], True)


def update_strips(place, blocks, mapping, coupling, inverse, parent, plan):
    order, pivots = coupling.shape
    counts = (plan.early + plan.n_parent + 1, len(plan.slot_pairs) - plan.early)
    return call(
        functools.partial(update_kernel, plan=plan),
        24,
        in_specs=[SMEM] * 3 + [HBM] * 3,
        out_specs=[VMEM] * 2,
        out_shape=[jax.ShapeDtypeStruct((plan.members, n, plan.strip, plan.blk), F32) for n in counts],
        scratch_shapes=[
            pltpu.VMEM(coupling.shape, F32),
            pltpu.VMEM(inverse.shape, F32),
            pltpu.VMEM(parent.shape, F32),
            pltpu.VMEM((order, pivots), BF16),
            pltpu.VMEM((order, pivots), BF16),
            pltpu.VMEM((order, order), F32),
            pltpu.SemaphoreType.DMA((4,)),
        ],
    )(place, blocks, mapping, *(in_hbm(v) for v in (coupling, inverse, parent)))


def merge_head_kernel(place, maps, table, early, head, token, total, *, plan):
    token[...] = jnp.zeros_like(token)
    base = plan.early

    @pl.when(place[1] == 0)
    def _():
        for e in range(plan.n_head):
            total[e] = early[0, base + e]

    @pl.when(place[1] != 0)
    def _():
        total[...] = jnp.zeros_like(total)

    def one(source, _):
        ids = [maps[source, s] + 1 for s in range(plan.per_tile)]
        for e, (i, j) in enumerate(plan.slot_pairs[: plan.early]):
            if i < plan.per_tile:
                total[table[ids[i], ids[j]]] -= early[source, e]
        return 0

    lax.fori_loop(0, plan.members, one, 0)
    head[...] = total[: plan.n_head]


def merge_head(place, maps, early, plan):
    tail = (plan.strip, plan.blk)
    table = np.minimum(plan.table, plan.n_head).astype(np.int32)
    return call(
        functools.partial(merge_head_kernel, plan=plan),
        6,
        in_specs=[SMEM] * 3 + [VMEM],
        out_specs=[VMEM] * 2,
        out_shape=[jax.ShapeDtypeStruct((plan.n_head,) + tail, F32), TOKEN],
        scratch_shapes=[pltpu.VMEM((plan.n_head + 1,) + tail, F32)],
    )(place, maps, jnp.asarray(table), early)


def merge_column_kernel(place, maps, table, early, after, column, total, *, plan):
    nb2 = len(plan.full)
    total[...] = jnp.zeros_like(total)
    base = plan.early

    @pl.when(place[1] == 0)
    def _():
        for r in range(1, plan.rows):
            for e in range(plan.first):
                total[(r - 1) * nb2 + e] = early[r * plan.near, base + e]

    for c in range(1, plan.rows):

        @pl.when(place[1] == c // plan.near)
        def _():
            for e in range(plan.first, nb2):
                total[(c - 1) * nb2 + e] = early[c % plan.near, base + e - plan.first]

    def one(source, _):
        ids = [maps[source, s] + 1 for s in range(plan.slots)]
        for e, (i, j) in enumerate(plan.slot_pairs[: plan.early]):
            if i > 0:
                total[table[ids[i], ids[j]]] -= early[source, e]
        return 0

    lax.fori_loop(0, plan.members, one, 0)
    column[...] = total[: plan.n_column]


def merge_column(place, maps, early, plan, after):
    tail = (plan.strip, plan.blk)
    first, last = plan.n_head, plan.n_head + plan.n_column
    inside = (plan.table >= first) & (plan.table < last)
    table = np.where(inside, plan.table - first, plan.n_column).astype(np.int32)
    return call(
        functools.partial(merge_column_kernel, plan=plan),
        8,
        in_specs=[SMEM] * 3 + [VMEM] + [AFTER],
        out_specs=VMEM,
        out_shape=jax.ShapeDtypeStruct((plan.n_column,) + tail, F32),
        scratch_shapes=[pltpu.VMEM((plan.n_column + 1,) + tail, F32)],
    )(place, maps, jnp.asarray(table), early, after)


def merge_rest_kernel(place, maps, table, begins, early, late, after, keep, send, token, total, *, plan):
    token[...] = jnp.zeros_like(token)
    total[...] = jnp.zeros_like(total)

    def one(source, _):
        ids = [maps[source, s] + 1 for s in range(plan.slots)]
        for e, (i, j) in enumerate(plan.slot_pairs):
            strip = early[source, e] if e < plan.early else late[source, e - plan.early]
            total[table[ids[i], ids[j]]] -= strip
        return 0

    lax.fori_loop(0, plan.members, one, 0)
    keep[...] = total[pl.ds(begins[place[1]], plan.window)]
    send[...] = total[pl.ds(begins[(place[1] + 1) % plan.far], plan.window)]


def merge_rest(place, maps, early, late, plan, after):
    first = plan.n_head + plan.n_column
    table = np.where(plan.table >= first, plan.table - first, plan.n_rest).astype(np.int32)
    shape = jax.ShapeDtypeStruct((plan.window, plan.strip, plan.blk), F32)
    return call(
        functools.partial(merge_rest_kernel, plan=plan),
        8,
        in_specs=[SMEM] * 4 + [VMEM] * 2 + [AFTER],
        out_specs=[VMEM] * 3,
        out_shape=[shape, shape, TOKEN],
        scratch_shapes=[pltpu.VMEM((plan.n_rest + 1, plan.strip, plan.blk), F32)],
    )(place, maps, jnp.asarray(table), jnp.asarray(np.array(plan.begins, np.int32)), early, late, after)


def column_kernel(place, mine, other, *refs, plan):
    sent, token, total, sems = refs[-4:]
    nb2 = len(plan.full)
    total[...] = mine[...] + other[...]
    copies = []
    for r in range(plan.rows):
        for n in range(plan.near):
            d = r * plan.near + n
            col = jnp.maximum(place[1] * plan.near + n - 1, 0)
            for k, first in enumerate((max(r - 1, 0) * nb2, col * nb2)):
                source, dest = total.at[pl.ds(first, nb2)], sent.at[d, pl.ds(k * nb2, nb2)]
                copies.append(pltpu.make_async_copy(source, dest, sems.at[2 * d + k]))
    for copy in copies:
        copy.start()
    token[...] = jnp.zeros_like(token)
    for copy in copies:
        copy.wait()


def column_strips(place, mine, other, plan, after):
    shape = (plan.members, 2 * len(plan.full)) + mine.shape[1:]
    return call(
        functools.partial(column_kernel, plan=plan),
        8,
        in_specs=[SMEM] + [VMEM] * 2 + [AFTER] * len(after),
        out_specs=[HBM, VMEM],
        out_shape=[pltpu.HBM(shape, F32), TOKEN],
        scratch_shapes=[pltpu.VMEM(mine.shape, F32), pltpu.SemaphoreType.DMA((2 * plan.members,))],
    )(place, mine, other, *after)


def rest_kernel(place, starts, mine, other, after, sent, token, total, sems, *, plan):
    nb2 = len(plan.full)
    total[...] = mine[...] + other[...]
    copies = []
    for r in range(plan.rows):
        for n in range(plan.near):
            d = r * plan.near + n
            source = total.at[pl.ds(starts[place[1] * plan.near + n, r], nb2)]
            copies.append(pltpu.make_async_copy(source, sent.at[d], sems.at[d]))
    for copy in copies:
        copy.start()
    token[...] = jnp.zeros_like(token)
    for copy in copies:
        copy.wait()


def rest_strips(place, mine, other, plan, after):
    cols = plan.near * plan.far
    nb2 = len(plan.full)
    starts = np.zeros((cols, plan.rows), np.int32)
    for c in range(1, cols):
        for r in range(1, plan.rows):
            starts[c, r] = min(plan.rest_at(r, c) - plan.begins[c // plan.near], plan.window - nb2)
    shape = (plan.members, nb2) + mine.shape[1:]
    return call(
        functools.partial(rest_kernel, plan=plan),
        4,
        in_specs=[SMEM] * 2 + [VMEM] * 2 + [AFTER],
        out_specs=[HBM, VMEM],
        out_shape=[pltpu.HBM(shape, F32), TOKEN],
        scratch_shapes=[pltpu.VMEM(mine.shape, F32), pltpu.SemaphoreType.DMA((plan.members,))],
    )(place, jnp.asarray(starts), mine, other, after)


def factor_block(a):
    step = 8
    count = a.shape[0] // step
    sub = lax.broadcasted_iota(jnp.int32, (step, a.shape[1]), 0)
    out = []
    for t in range(count):
        top = a[:step]
        row = lambda v, q: jnp.broadcast_to(v[q : q + 1], v.shape)
        col = lambda v, q: jnp.broadcast_to(v[:, step * t + q : step * t + q + 1], v.shape)
        cols = [col(top, q) for q in range(step)]
        pivot = {(p, q): row(cols[q], p) for q in range(step) for p in range(q, step)}
        scale, low = [], {}
        for q in range(step):
            scale.append(lax.rsqrt(pivot[q, q]))
            for p in range(q + 1, step):
                low[p, q] = pivot[p, q] * scale[q]
            for p in range(q + 1, step):
                for m in range(q + 1, p + 1):
                    pivot[p, m] = pivot[p, m] - low[p, q] * low[m, q]
        rows = [row(top, q) for q in range(step)]
        u = []
        for q in range(step):
            u.append(rows[q] * scale[q])
            for p in range(q + 1, step):
                rows[p] = rows[p] - low[p, q] * u[q]
        done = u[0]
        for q in range(1, step):
            done = jnp.where(sub == q, u[q], done)
        out.append(done)
        if t == count - 1:
            break
        for q in reversed(range(step)):
            u[q] = u[q] * scale[q]
            for p in range(q):
                u[p] = u[p] - low[q, p] * u[q]
        a = a[step:]
        cols = [col(a, q) for q in range(step)]
        for q in range(step):
            a = a - cols[q] * jnp.broadcast_to(u[q][:1], a.shape)
    return jnp.concatenate(out, 0)


def cholesky_kernel(place, *refs, plan):
    heads, (keep, _, l_ref, x_ref, brought, token, s, sem) = refs[: plan.rows], refs[plan.rows :]
    copy = pltpu.make_async_copy(keep, brought, sem)
    copy.start()
    token[...] = jnp.zeros_like(token)
    n = l_ref.shape[0]
    blk, nb = plan.blk, plan.blk // 2
    l_ref[...] = jnp.zeros_like(l_ref)
    x_ref[...] = jnp.zeros_like(x_ref)
    for k, ref in enumerate(heads):
        for m in range(plan.near):
            member = (place[0] ^ k) * plan.near + (place[2] ^ m)
            for e, (i, j) in enumerate(plan.lower):
                top = pl.multiple_of(i * blk + member * plan.strip, plan.strip)
                s[pl.ds(top, plan.strip), j * blk : (j + 1) * blk] = ref[m, e]
    for i, j in plan.lower:
        if i > j:
            s[j * blk : (j + 1) * blk, i * blk : (i + 1) * blk] = s[i * blk : (i + 1) * blk, j * blk : (j + 1) * blk].T
    r, c = (lax.broadcasted_iota(jnp.int32, (nb, nb), d) for d in range(2))
    for off in range(0, n, nb):
        end = off + nb
        both = factor_block(jnp.concatenate([s[off:end, off:end], (r == c).astype(F32)], 1))
        w = both[:, nb:]
        l_ref[off:end, off:end] = jnp.where(r >= c, both[:, :nb].T, 0.0)
        x_ref[off:end, off:end] = w
        if off:
            x_ref[off:end, :off] = dot_nn(w, x_ref[off:end, :off])
        if end < n:
            below = dot_nt(s[end:, off:end], w)
            s[end:, end:] -= dot_nt(below, below)
            l_ref[end:, off:end] = below
            x_ref[end:, :end] -= dot_nn(below, x_ref[off:end, :end])
    copy.wait()


def cholesky(place, heads, keep, n, plan, after):
    square = jax.ShapeDtypeStruct((n, n), F32)
    return call(
        functools.partial(cholesky_kernel, plan=plan),
        12,
        in_specs=[SMEM] + [VMEM] * plan.rows + [HBM, AFTER],
        out_specs=[VMEM] * 4,
        out_shape=[square, square, jax.ShapeDtypeStruct(keep.shape, F32), TOKEN],
        scratch_shapes=[pltpu.VMEM((n, n), F32), pltpu.SemaphoreType.DMA(())],
    )(place, *heads, in_hbm(keep), after)


def put(ref, source, first, blocks, plan):
    blk, size = plan.blk, plan.strip
    for e, (a, b) in enumerate(blocks):
        for d in range(plan.members):
            top = a * blk + d * size
            ref[top : top + size, b * blk : (b + 1) * blk] = source[d, first + e]


def panel_kernel(place, columns, parent, l_ref, x_ref, after, out, a_row, a_col, *, plan):
    nb2 = len(plan.full)
    row = place[0]
    col = place[1] * plan.near + place[2]

    @pl.when((row == 0) & (col == 0))
    def _():
        out[...] = l_ref[...]

    @pl.when((row == 0) & (col > 0))
    def _():
        put(a_col, columns, nb2, plan.full, plan)
        out[...] = a_col[...].T

    @pl.when(row > 0)
    def _():
        put(a_row, columns, 0, plan.full, plan)
        a_row[...] = dot_nt(a_row[...], x_ref[...])

    @pl.when((row > 0) & (col == 0))
    def _():
        out[...] = a_row[...]

    @pl.when((row > 0) & (col == row))
    def _():
        pair = split(a_row[...])
        out[...] = parent[...] - dot3(pair, pair)

    @pl.when((row > 0) & (col > 0) & (col != row))
    def _():
        put(a_col, columns, nb2, plan.full, plan)
        out[...] = parent[...] - dot3(split(a_row[...]), split(dot_nt(a_col[...], x_ref[...])))


def panel(place, columns, parent, l, x, plan, after):
    return call(
        functools.partial(panel_kernel, plan=plan),
        12,
        in_specs=[SMEM] + [VMEM] * 4 + [AFTER],
        out_specs=VMEM,
        out_shape=jax.ShapeDtypeStruct(parent.shape, F32),
        scratch_shapes=[pltpu.VMEM(parent.shape, F32)] * 2,
    )(place, columns, parent, l, x, after)


def finish_kernel(place, rests_in, base_in, out_ref, tile, rests, base, out, sems, *, plan):
    blk, nb = plan.blk, plan.per_tile
    copies = [pltpu.make_async_copy(base_in, base, sems.at[0]), pltpu.make_async_copy(rests_in, rests, sems.at[1])]
    for copy in copies:
        copy.start()
    for copy in copies:
        copy.wait()
    row = place[0]
    col = place[1] * plan.near + place[2]

    def write(value):
        parts = []
        for a in range(nb):
            rows = slice(a * blk, (a + 1) * blk)
            out[rows, :] = value(rows)
            window = pl.ds(a * blk, blk)
            parts.append(pltpu.make_async_copy(out.at[window], out_ref.at[window], sems.at[2 + a]))
            parts[-1].start()
        for copy in parts:
            copy.wait()

    @pl.when((row == 0) | (col == 0))
    def _():
        write(lambda rows: base[rows, :])

    @pl.when((row > 0) & (col == row))
    def _():
        put(tile, rests, 0, plan.lower, plan)
        for a, b in plan.lower:
            if a > b:
                tile[b * blk : (b + 1) * blk, a * blk : (a + 1) * blk] = tile[
                    a * blk : (a + 1) * blk, b * blk : (b + 1) * blk
                ].T
        write(lambda rows: base[rows, :] + tile[rows, :])

    @pl.when((row > col) & (col > 0))
    def _():
        put(tile, rests, 0, plan.full, plan)
        write(lambda rows: base[rows, :] + tile[rows, :])

    @pl.when((row > 0) & (row < col))
    def _():
        put(tile, rests, 0, plan.full, plan)
        write(lambda rows: base[rows, :] + tile[:, rows].T)


def finish(place, rests, base, plan):
    return call(
        functools.partial(finish_kernel, plan=plan),
        10,
        in_specs=[SMEM] + [HBM] * 2,
        out_specs=HBM,
        out_shape=jax.ShapeDtypeStruct(base.shape, F32),
        scratch_shapes=[
            pltpu.VMEM(base.shape, F32),
            pltpu.VMEM(rests.shape, F32),
            pltpu.VMEM(base.shape, F32),
            pltpu.VMEM(base.shape, F32),
            pltpu.SemaphoreType.DMA((2 + plan.per_tile,)),
        ],
    )(place, in_hbm(rests), in_hbm(base))


def all_to_all(x):
    return lax.all_to_all(x, GROUP, 0, 0, tiled=True)


def across(x, plan):
    others = [
        lax.ppermute(x, "far", [(f, (f + by) % plan.far) for f in range(plan.far)]) for by in range(1, plan.far)
    ]
    return functools.reduce(jnp.add, others)


def spread_head(head, plan):
    cols = plan.near * plan.far
    got = [head] + [lax.ppermute(head, ("far", "near"), [(d, d ^ k) for d in range(cols)]) for k in range(1, cols)]
    pair = jnp.stack([sum(got[m + plan.near :: plan.near], got[m]) for m in range(plan.near)])
    return [pair] + [lax.ppermute(pair, "prow", [(d, d ^ k) for d in range(plan.rows)]) for k in range(1, plan.rows)]


def body(child_inverse, child_coupling, child_blocks, child_map, parent_front, plan):
    place = jnp.stack([lax.axis_index(a) for a in ("prow", "far", "near")]).astype(jnp.int32)
    early, late = update_strips(
        place, child_blocks, child_map, child_coupling[0], child_inverse[0], parent_front, plan
    )
    early = all_to_all(early)
    late = all_to_all(late)
    maps = early[:, -1, 0, : plan.slots].astype(jnp.int32)
    head, token = merge_head(place, maps, early, plan)
    heads = spread_head(head, plan)
    column = merge_column(place, maps, early, plan, token)
    far_column = across(column, plan)
    keep, send, token = merge_rest(place, maps, early, late, plan, heads[0])
    sent, token = column_strips(place, column, far_column, plan, [token] + heads[1:])
    columns = all_to_all(sent)
    l, x, keep, token = cholesky(place, heads, keep, parent_front.shape[0], plan, token)
    sent, token = rest_strips(place, keep, across(send, plan), plan, token)
    base = panel(place, columns, parent_front, l, x, plan, token)
    rests = all_to_all(sent)
    return finish(place, rests, base, plan)


def solution(mesh):
    rows, cols = mesh.shape["prow"], mesh.shape["pcol"]
    near = 2 if cols % 2 == 0 else 1
    fine = Mesh(
        mesh.devices.reshape(mesh.shape["leaf"], rows, cols // near, near), ("leaf", "prow", "far", "near")
    )
    device = P(("leaf", "prow", "far", "near"))

    def run(child_inverse, child_coupling, child_blocks, child_map, parent_front):
        slots = child_map.shape[1]
        blk = child_coupling.shape[1] // slots
        plan = Plan(rows, near, cols // near, parent_front.shape[1] // cols // blk, slots, blk)
        tile = P(("leaf", "prow"), ("far", "near"))
        return jax.shard_map(
            functools.partial(body, plan=plan),
            mesh=fine,
            in_specs=(device, device, device, device, tile),
            out_specs=tile,
            check_vma=False,
        )(child_inverse, child_coupling, child_blocks, child_map, parent_front)

    return run
```

```python
import functools

import jax
import jax.numpy as jnp
import numpy as np
from jax import lax
from jax.experimental import pallas as pl
from jax.experimental.pallas import tpu as pltpu
from jax.sharding import Mesh
from jax.sharding import PartitionSpec as P

F32 = jnp.float32
BF16 = jnp.bfloat16
SMEM = pl.BlockSpec(memory_space=pltpu.SMEM)
VMEM = pl.BlockSpec(memory_space=pltpu.VMEM)
HBM = pl.BlockSpec(memory_space=pltpu.HBM)
AFTER = pl.BlockSpec(memory_space=pl.ANY)
GROUP = ("prow", "near")


def in_hbm(x):
    return pltpu.with_memory_space_constraint(x, pltpu.HBM)


def in_vmem(x):
    return pltpu.with_memory_space_constraint(x, pltpu.VMEM)


TOKEN = jax.ShapeDtypeStruct((8, 128), F32)


def call(kernel, megabytes, **kwargs):
    return pl.pallas_call(
        kernel,
        compiler_params=pltpu.CompilerParams(vmem_limit_bytes=megabytes * 2**20),
        cost_estimate=pl.CostEstimate(flops=1, bytes_accessed=1, transcendentals=0),
        **kwargs,
    )


class Plan:
    def __init__(self, rows, near, far, per_tile, slots, blk):
        self.rows, self.near, self.far = rows, near, far
        self.per_tile, self.slots, self.blk = per_tile, slots, blk
        self.members = rows * near
        self.strip = blk // self.members
        nb = per_tile
        self.lower = [(a, b) for b in range(nb) for a in range(b, nb)]
        self.full = [(a, b) for a in range(nb) for b in range(nb)]
        self.pairs = [(h, l) for h in range(1, rows) for l in range(1, h)]
        self.n_head = len(self.lower)
        self.n_column = (rows - 1) * nb * nb
        tiles = [(r, r) for r in range(1, rows)] + self.pairs
        need = {t: sorted({c // near for c in t}) for t in tiles}
        tiles.sort(key=lambda t: need[t])
        size = {t: len(self.lower) if t[0] == t[1] else nb * nb for t in tiles}
        self.starts = {t: sum(size[u] for u in tiles[:k]) for k, t in enumerate(tiles)}
        self.n_rest = sum(size.values())
        spans = []
        for f in range(far):
            held = [t for t in tiles if f in need[t]]
            spans.append((min(self.starts[t] for t in held), max(self.starts[t] + size[t] for t in held)))
        self.window = max(end - begin for begin, end in spans)
        self.begins = [min(begin, self.n_rest - self.window) for begin, _ in spans]
        self.total = self.n_head + self.n_column + self.n_rest
        self.first = len(self.full) // 2
        self.n_parent = max(len(self.lower), len(self.full) - self.first)
        self.slot_pairs = [(i, j) for j in range(slots) for i in range(j, slots)]
        self.early = sum(j < nb for _, j in self.slot_pairs)
        table = np.full((rows * nb + 1, rows * nb + 1), self.total, np.int32)
        rest = self.n_head + self.n_column
        for r in range(rows):
            for e, (a, b) in enumerate(self.lower):
                at = e if r == 0 else rest + self.rest_at(r, r) + e
                table[r * nb + a + 1, r * nb + b + 1] = at
        for h in range(1, rows):
            for l in range(h):
                for e, (a, b) in enumerate(self.full):
                    at = self.n_head + (h - 1) * nb * nb + e if l == 0 else rest + self.rest_at(h, l) + e
                    table[h * nb + a + 1, l * nb + b + 1] = at
        self.table = table

    def rest_at(self, r, c):
        if r == 0 or c == 0:
            return 0
        return self.starts[max(r, c), min(r, c)]


def split(x):
    high = x.astype(BF16)
    return high, (x - high.astype(F32)).astype(BF16)


def dot3(a, b):
    dims = (((1,), (1,)), ((), ()))
    dot = lambda u, v: lax.dot_general(u, v, dims, preferred_element_type=F32)
    return dot(a[0], b[0]) + (dot(a[0], b[1]) + dot(a[1], b[0]))


def dot_nt(a, b):
    return lax.dot_general(
        a, b, (((1,), (1,)), ((), ())), precision=lax.Precision.HIGHEST, preferred_element_type=F32
    )


def dot_nn(a, b):
    return lax.dot_general(
        a, b, (((1,), (0,)), ((), ())), precision=lax.Precision.HIGHEST, preferred_element_type=F32
    )


def update_kernel(
    place, blocks, mapping_in, coupling, inverse, parent, early, late, left, right, own, high, low, update, mapping, sems, *, plan
):
    blk, size = plan.blk, plan.strip
    order = coupling.shape[0]
    width = order // 2
    starts = [0, width]
    copies = [pltpu.make_async_copy(inverse, right, sems.at[0])]
    for k, start in enumerate(starts):
        window = pl.ds(start, width)
        copies.append(pltpu.make_async_copy(coupling.at[window], left.at[window], sems.at[k + 1]))
    copies.append(pltpu.make_async_copy(parent, own, sems.at[len(starts) + 1]))
    ids = pltpu.make_async_copy(mapping_in, mapping, sems.at[len(starts) + 2])
    ids.start()
    for copy in copies:
        copy.start()
    base = plan.early
    copies[0].wait()
    factor_of = split(right[...])
    for k, start in enumerate(starts):
        window = slice(start, start + width)
        copies[k + 1].wait()
        rows = start + lax.broadcasted_iota(jnp.int32, (width, 1), 0)
        masked = jnp.where(rows < blocks[0] * blk, left[window, :], 0.0)
        high[window, :], low[window, :] = split(dot3(split(masked), factor_of))
    panel = 2 * blk
    for start in range(0, order, panel):
        cols = slice(start, start + panel)
        update[start:, cols] = dot3((high[start:, :], low[start:, :]), (high[cols, :], low[cols, :]))
    for e, (i, j) in enumerate(plan.slot_pairs):
        for d in range(plan.members):
            top = i * blk + d * size
            strip = update[top : top + size, j * blk : (j + 1) * blk]
            if e < plan.early:
                early[d, e] = strip
            else:
                late[d, e - plan.early] = strip

    ids.wait()
    lanes = lax.broadcasted_iota(jnp.int32, (size, blk), 1)
    coded = jnp.zeros((size, blk), F32)
    for s in range(plan.slots):
        coded = jnp.where(lanes == s, mapping[0, s].astype(F32), coded)
    for d in range(plan.members):
        early[d, base + plan.n_parent] = coded
    copies[-1].wait()
    row, col = place[0], place[1] * plan.near + place[2]

    def send(blocks, transposed):
        for e, (a, b) in enumerate(blocks):
            p, q = (b, a) if transposed else (a, b)
            block = own[p * blk : (p + 1) * blk, q * blk : (q + 1) * blk]
            block = block.T if transposed else block
            for d in range(plan.members):
                early[d, base + e] = block[d * size : (d + 1) * size]

    @pl.when((row == 0) & (col == 0))
    def _():
        send(plan.lower, False)

    @pl.when((row > 0) & (col == 0))
    def _():
        send(plan.full[: plan.first], False)

    @pl.when((row == 0) & (col > 0))
    def _():
        send(plan.full[plan.first :], True)


def update_strips(place, blocks, mapping, coupling, inverse, parent, plan):
    order, pivots = coupling.shape
    counts = (plan.early + plan.n_parent + 1, len(plan.slot_pairs) - plan.early)
    return call(
        functools.partial(update_kernel, plan=plan),
        24,
        in_specs=[SMEM] * 2 + [HBM] * 4,
        out_specs=[VMEM] * 2,
        out_shape=[jax.ShapeDtypeStruct((plan.members, n, plan.strip, plan.blk), F32) for n in counts],
        scratch_shapes=[
            pltpu.VMEM(coupling.shape, F32),
            pltpu.VMEM(inverse.shape, F32),
            pltpu.VMEM(parent.shape, F32),
            pltpu.VMEM((order, pivots), BF16),
            pltpu.VMEM((order, pivots), BF16),
            pltpu.VMEM((order, order), F32),
            pltpu.SMEM(mapping.shape, jnp.int32),
            pltpu.SemaphoreType.DMA((5,)),
        ],
    )(place, blocks, *(in_hbm(v) for v in (mapping, coupling, inverse, parent)))


def merge_head_kernel(place, maps, table, early, head, token, total, *, plan):
    token[...] = jnp.zeros_like(token)
    base = plan.early

    @pl.when(place[1] == 0)
    def _():
        for e in range(plan.n_head):
            total[e] = early[0, base + e]

    @pl.when(place[1] != 0)
    def _():
        total[...] = jnp.zeros_like(total)

    def one(source, _):
        ids = [maps[source, s] + 1 for s in range(plan.per_tile)]
        for e, (i, j) in enumerate(plan.slot_pairs[: plan.early]):
            if i < plan.per_tile:
                total[table[ids[i], ids[j]]] -= early[source, e]
        return 0

    lax.fori_loop(0, plan.members, one, 0)
    head[...] = total[: plan.n_head]


def merge_head(place, maps, early, plan):
    tail = (plan.strip, plan.blk)
    table = np.minimum(plan.table, plan.n_head).astype(np.int32)
    return call(
        functools.partial(merge_head_kernel, plan=plan),
        6,
        in_specs=[SMEM] * 3 + [VMEM],
        out_specs=[VMEM] * 2,
        out_shape=[jax.ShapeDtypeStruct((plan.n_head,) + tail, F32), TOKEN],
        scratch_shapes=[pltpu.VMEM((plan.n_head + 1,) + tail, F32)],
    )(place, maps, jnp.asarray(table), early)


def merge_column_kernel(place, maps, table, early, after, column, total, *, plan):
    nb2 = len(plan.full)
    total[...] = jnp.zeros_like(total)
    base = plan.early

    @pl.when(place[1] == 0)
    def _():
        for r in range(1, plan.rows):
            for e in range(plan.first):
                total[(r - 1) * nb2 + e] = early[r * plan.near, base + e]

    for c in range(1, plan.rows):

        @pl.when(place[1] == c // plan.near)
        def _():
            for e in range(plan.first, nb2):
                total[(c - 1) * nb2 + e] = early[c % plan.near, base + e - plan.first]

    def one(source, _):
        ids = [maps[source, s] + 1 for s in range(plan.slots)]
        for e, (i, j) in enumerate(plan.slot_pairs[: plan.early]):
            if i > 0:
                total[table[ids[i], ids[j]]] -= early[source, e]
        return 0

    lax.fori_loop(0, plan.members, one, 0)
    column[...] = total[: plan.n_column]


def merge_column(place, maps, early, plan, after):
    tail = (plan.strip, plan.blk)
    first, last = plan.n_head, plan.n_head + plan.n_column
    inside = (plan.table >= first) & (plan.table < last)
    table = np.where(inside, plan.table - first, plan.n_column).astype(np.int32)
    return call(
        functools.partial(merge_column_kernel, plan=plan),
        8,
        in_specs=[SMEM] * 3 + [VMEM] + [AFTER],
        out_specs=VMEM,
        out_shape=jax.ShapeDtypeStruct((plan.n_column,) + tail, F32),
        scratch_shapes=[pltpu.VMEM((plan.n_column + 1,) + tail, F32)],
    )(place, maps, jnp.asarray(table), early, after)


def merge_rest_kernel(place, maps, table, begins, early, late, after, keep, send, token, total, *, plan):
    token[...] = jnp.zeros_like(token)
    total[...] = jnp.zeros_like(total)

    def one(source, _):
        ids = [maps[source, s] + 1 for s in range(plan.slots)]
        for e, (i, j) in enumerate(plan.slot_pairs):
            strip = early[source, e] if e < plan.early else late[source, e - plan.early]
            total[table[ids[i], ids[j]]] -= strip
        return 0

    lax.fori_loop(0, plan.members, one, 0)
    keep[...] = total[pl.ds(begins[place[1]], plan.window)]
    send[...] = total[pl.ds(begins[(place[1] + 1) % plan.far], plan.window)]


def merge_rest(place, maps, early, late, plan, after):
    first = plan.n_head + plan.n_column
    table = np.where(plan.table >= first, plan.table - first, plan.n_rest).astype(np.int32)
    shape = jax.ShapeDtypeStruct((plan.window, plan.strip, plan.blk), F32)
    return call(
        functools.partial(merge_rest_kernel, plan=plan),
        8,
        in_specs=[SMEM] * 4 + [VMEM] * 2 + [AFTER],
        out_specs=[VMEM] * 3,
        out_shape=[shape, shape, TOKEN],
        scratch_shapes=[pltpu.VMEM((plan.n_rest + 1, plan.strip, plan.blk), F32)],
    )(place, maps, jnp.asarray(table), jnp.asarray(np.array(plan.begins, np.int32)), early, late, after)


def column_kernel(place, mine, other, *refs, plan):
    sent, token, total, sems = refs[-4:]
    nb2 = len(plan.full)
    total[...] = mine[...] + other[...]
    copies = []
    for r in range(plan.rows):
        for n in range(plan.near):
            d = r * plan.near + n
            col = jnp.maximum(place[1] * plan.near + n - 1, 0)
            for k, first in enumerate((max(r - 1, 0) * nb2, col * nb2)):
                source, dest = total.at[pl.ds(first, nb2)], sent.at[d, pl.ds(k * nb2, nb2)]
                copies.append(pltpu.make_async_copy(source, dest, sems.at[2 * d + k]))
    for copy in copies:
        copy.start()
    token[...] = jnp.zeros_like(token)
    for copy in copies:
        copy.wait()


def column_strips(place, mine, other, plan, after):
    shape = (plan.members, 2 * len(plan.full)) + mine.shape[1:]
    return call(
        functools.partial(column_kernel, plan=plan),
        8,
        in_specs=[SMEM] + [VMEM] * 2 + [AFTER] * len(after),
        out_specs=[HBM, VMEM],
        out_shape=[pltpu.HBM(shape, F32), TOKEN],
        scratch_shapes=[pltpu.VMEM(mine.shape, F32), pltpu.SemaphoreType.DMA((2 * plan.members,))],
    )(place, mine, other, *after)


def rest_kernel(place, starts, mine, other, after, sent, token, total, sems, *, plan):
    nb2 = len(plan.full)
    total[...] = mine[...] + other[...]
    copies = []
    for r in range(plan.rows):
        for n in range(plan.near):
            d = r * plan.near + n
            source = total.at[pl.ds(starts[place[1] * plan.near + n, r], nb2)]
            copies.append(pltpu.make_async_copy(source, sent.at[d], sems.at[d]))
    for copy in copies:
        copy.start()
    token[...] = jnp.zeros_like(token)
    for copy in copies:
        copy.wait()


def rest_strips(place, mine, other, plan, after):
    cols = plan.near * plan.far
    nb2 = len(plan.full)
    starts = np.zeros((cols, plan.rows), np.int32)
    for c in range(1, cols):
        for r in range(1, plan.rows):
            starts[c, r] = min(plan.rest_at(r, c) - plan.begins[c // plan.near], plan.window - nb2)
    shape = (plan.members, nb2) + mine.shape[1:]
    return call(
        functools.partial(rest_kernel, plan=plan),
        4,
        in_specs=[SMEM] * 2 + [VMEM] * 2 + [AFTER],
        out_specs=[HBM, VMEM],
        out_shape=[pltpu.HBM(shape, F32), TOKEN],
        scratch_shapes=[pltpu.VMEM(mine.shape, F32), pltpu.SemaphoreType.DMA((plan.members,))],
    )(place, jnp.asarray(starts), mine, other, after)


def factor_block(a):
    step = 8
    count = a.shape[0] // step
    sub = lax.broadcasted_iota(jnp.int32, (step, a.shape[1]), 0)
    out = []
    for t in range(count):
        top = a[:step]
        row = lambda v, q: jnp.broadcast_to(v[q : q + 1], v.shape)
        col = lambda v, q: jnp.broadcast_to(v[:, step * t + q : step * t + q + 1], v.shape)
        cols = [col(top, q) for q in range(step)]
        pivot = {(p, q): row(cols[q], p) for q in range(step) for p in range(q, step)}
        scale, low = [], {}
        for q in range(step):
            scale.append(lax.rsqrt(pivot[q, q]))
            for p in range(q + 1, step):
                low[p, q] = pivot[p, q] * scale[q]
            for p in range(q + 1, step):
                for m in range(q + 1, p + 1):
                    pivot[p, m] = pivot[p, m] - low[p, q] * low[m, q]
        rows = [row(top, q) for q in range(step)]
        u = []
        for q in range(step):
            u.append(rows[q] * scale[q])
            for p in range(q + 1, step):
                rows[p] = rows[p] - low[p, q] * u[q]
        done = u[0]
        for q in range(1, step):
            done = jnp.where(sub == q, u[q], done)
        out.append(done)
        if t == count - 1:
            break
        for q in reversed(range(step)):
            u[q] = u[q] * scale[q]
            for p in range(q):
                u[p] = u[p] - low[q, p] * u[q]
        a = a[step:]
        cols = [col(a, q) for q in range(step)]
        for q in range(step):
            a = a - cols[q] * jnp.broadcast_to(u[q][:1], a.shape)
    return jnp.concatenate(out, 0)


def cholesky_kernel(place, *refs, plan):
    heads, (keep, _, l_ref, x_ref, brought, token, s, sem) = refs[: plan.rows], refs[plan.rows :]
    copy = pltpu.make_async_copy(keep, brought, sem)
    copy.start()
    token[...] = jnp.zeros_like(token)
    n = l_ref.shape[0]
    blk, nb = plan.blk, plan.blk // 2
    l_ref[...] = jnp.zeros_like(l_ref)
    x_ref[...] = jnp.zeros_like(x_ref)
    for k, ref in enumerate(heads):
        for m in range(plan.near):
            member = (place[0] ^ k) * plan.near + (place[2] ^ m)
            for e, (i, j) in enumerate(plan.lower):
                top = pl.multiple_of(i * blk + member * plan.strip, plan.strip)
                s[pl.ds(top, plan.strip), j * blk : (j + 1) * blk] = ref[m, e]
    for i, j in plan.lower:
        if i > j:
            s[j * blk : (j + 1) * blk, i * blk : (i + 1) * blk] = s[i * blk : (i + 1) * blk, j * blk : (j + 1) * blk].T
    r, c = (lax.broadcasted_iota(jnp.int32, (nb, nb), d) for d in range(2))
    for off in range(0, n, nb):
        end = off + nb
        both = factor_block(jnp.concatenate([s[off:end, off:end], (r == c).astype(F32)], 1))
        w = both[:, nb:]
        if end < n:
            below = dot_nt(s[end:, off:end], w)
            s[end : end + nb, end : end + nb] -= dot_nt(below[:nb], below[:nb])
            if end + nb < n:
                s[end + nb :, end:] -= dot_nt(below[nb:], below)
            l_ref[end:, off:end] = below
        l_ref[off:end, off:end] = jnp.where(r >= c, both[:, :nb].T, 0.0)
        x_ref[off:end, off:end] = w
        if off:
            x_ref[off:end, :off] = dot_nn(w, x_ref[off:end, :off])
        if end < n:
            x_ref[end:, :end] -= dot_nn(below, x_ref[off:end, :end])
    copy.wait()


def cholesky(place, heads, keep, n, plan, after):
    square = jax.ShapeDtypeStruct((n, n), F32)
    return call(
        functools.partial(cholesky_kernel, plan=plan),
        12,
        in_specs=[SMEM] + [VMEM] * plan.rows + [HBM, AFTER],
        out_specs=[VMEM] * 4,
        out_shape=[square, square, jax.ShapeDtypeStruct(keep.shape, F32), TOKEN],
        scratch_shapes=[pltpu.VMEM((n, n), F32), pltpu.SemaphoreType.DMA(())],
    )(place, *heads, in_hbm(keep), after)


def put(ref, source, first, blocks, plan):
    blk, size = plan.blk, plan.strip
    for e, (a, b) in enumerate(blocks):
        for d in range(plan.members):
            top = a * blk + d * size
            ref[top : top + size, b * blk : (b + 1) * blk] = source[d, first + e]


def panel_kernel(place, columns, parent, l_ref, x_ref, after, out, a_row, a_col, *, plan):
    nb2 = len(plan.full)
    row = place[0]
    col = place[1] * plan.near + place[2]

    @pl.when((row == 0) & (col == 0))
    def _():
        out[...] = l_ref[...]

    @pl.when((row == 0) & (col > 0))
    def _():
        put(a_col, columns, nb2, plan.full, plan)
        out[...] = a_col[...].T

    @pl.when(row > 0)
    def _():
        put(a_row, columns, 0, plan.full, plan)
        a_row[...] = dot_nt(a_row[...], x_ref[...])

    @pl.when((row > 0) & (col == 0))
    def _():
        out[...] = a_row[...]

    @pl.when((row > 0) & (col == row))
    def _():
        pair = split(a_row[...])
        out[...] = parent[...] - dot3(pair, pair)

    @pl.when((row > 0) & (col > 0) & (col != row))
    def _():
        put(a_col, columns, nb2, plan.full, plan)
        out[...] = parent[...] - dot3(split(a_row[...]), split(dot_nt(a_col[...], x_ref[...])))


def panel(place, columns, parent, l, x, plan, after):
    return call(
        functools.partial(panel_kernel, plan=plan),
        12,
        in_specs=[SMEM] + [VMEM] * 4 + [AFTER],
        out_specs=VMEM,
        out_shape=jax.ShapeDtypeStruct(parent.shape, F32),
        scratch_shapes=[pltpu.VMEM(parent.shape, F32)] * 2,
    )(place, columns, parent, l, x, after)


def finish_kernel(place, rests_in, base_in, out_ref, tile, rests, base, out, sems, *, plan):
    blk, nb = plan.blk, plan.per_tile
    copies = [pltpu.make_async_copy(base_in, base, sems.at[0]), pltpu.make_async_copy(rests_in, rests, sems.at[1])]
    for copy in copies:
        copy.start()
    for copy in copies:
        copy.wait()
    row = place[0]
    col = place[1] * plan.near + place[2]

    def write(value):
        parts = []
        for a in range(nb):
            rows = slice(a * blk, (a + 1) * blk)
            out[rows, :] = value(rows)
            window = pl.ds(a * blk, blk)
            parts.append(pltpu.make_async_copy(out.at[window], out_ref.at[window], sems.at[2 + a]))
            parts[-1].start()
        for copy in parts:
            copy.wait()

    @pl.when((row == 0) | (col == 0))
    def _():
        write(lambda rows: base[rows, :])

    @pl.when((row > 0) & (col == row))
    def _():
        put(tile, rests, 0, plan.lower, plan)
        for a, b in plan.lower:
            if a > b:
                tile[b * blk : (b + 1) * blk, a * blk : (a + 1) * blk] = tile[
                    a * blk : (a + 1) * blk, b * blk : (b + 1) * blk
                ].T
        write(lambda rows: base[rows, :] + tile[rows, :])

    @pl.when((row > col) & (col > 0))
    def _():
        put(tile, rests, 0, plan.full, plan)
        write(lambda rows: base[rows, :] + tile[rows, :])

    @pl.when((row > 0) & (row < col))
    def _():
        put(tile, rests, 0, plan.full, plan)
        write(lambda rows: base[rows, :] + tile[:, rows].T)


def finish(place, rests, base, plan):
    return call(
        functools.partial(finish_kernel, plan=plan),
        10,
        in_specs=[SMEM] + [HBM] * 2,
        out_specs=HBM,
        out_shape=jax.ShapeDtypeStruct(base.shape, F32),
        scratch_shapes=[
            pltpu.VMEM(base.shape, F32),
            pltpu.VMEM(rests.shape, F32),
            pltpu.VMEM(base.shape, F32),
            pltpu.VMEM(base.shape, F32),
            pltpu.SemaphoreType.DMA((2 + plan.per_tile,)),
        ],
    )(place, in_hbm(rests), in_hbm(base))


def all_to_all(x):
    return lax.all_to_all(x, GROUP, 0, 0, tiled=True)


def across(x, plan):
    others = [
        lax.ppermute(x, "far", [(f, (f + by) % plan.far) for f in range(plan.far)]) for by in range(1, plan.far)
    ]
    return functools.reduce(jnp.add, others)


def spread_head(head, plan):
    cols = plan.near * plan.far
    got = [head] + [lax.ppermute(head, ("far", "near"), [(d, d ^ k) for d in range(cols)]) for k in range(1, cols)]
    pair = jnp.stack([sum(got[m + plan.near :: plan.near], got[m]) for m in range(plan.near)])
    return [pair] + [lax.ppermute(pair, "prow", [(d, d ^ k) for d in range(plan.rows)]) for k in range(1, plan.rows)]


def body(child_inverse, child_coupling, child_blocks, child_map, parent_front, plan):
    place = jnp.stack([lax.axis_index(a) for a in ("prow", "far", "near")]).astype(jnp.int32)
    early, late = update_strips(
        place, child_blocks, child_map, child_coupling[0], child_inverse[0], parent_front, plan
    )
    early = all_to_all(early)
    late = all_to_all(late)
    maps = early[:, -1, 0, : plan.slots].astype(jnp.int32)
    head, token = merge_head(place, maps, early, plan)
    heads = spread_head(head, plan)
    column = merge_column(place, maps, early, plan, token)
    far_column = across(column, plan)
    keep, send, token = merge_rest(place, maps, early, late, plan, heads[0])
    sent, token = column_strips(place, column, far_column, plan, [token] + heads[1:])
    columns = all_to_all(sent)
    l, x, keep, token = cholesky(place, heads, keep, parent_front.shape[0], plan, token)
    sent, token = rest_strips(place, keep, across(send, plan), plan, token)
    base = panel(place, columns, parent_front, l, x, plan, token)
    rests = all_to_all(sent)
    return finish(place, rests, base, plan)


def solution(mesh):
    rows, cols = mesh.shape["prow"], mesh.shape["pcol"]
    near = 2 if cols % 2 == 0 else 1
    fine = Mesh(
        mesh.devices.reshape(mesh.shape["leaf"], rows, cols // near, near), ("leaf", "prow", "far", "near")
    )
    device = P(("leaf", "prow", "far", "near"))

    def run(child_inverse, child_coupling, child_blocks, child_map, parent_front):
        slots = child_map.shape[1]
        blk = child_coupling.shape[1] // slots
        plan = Plan(rows, near, cols // near, parent_front.shape[1] // cols // blk, slots, blk)
        tile = P(("leaf", "prow"), ("far", "near"))
        return jax.shard_map(
            functools.partial(body, plan=plan),
            mesh=fine,
            in_specs=(device, device, device, device, tile),
            out_specs=tile,
            check_vma=False,
        )(child_inverse, child_coupling, child_blocks, child_map, parent_front)

    return run
```
